32 devices in a mesh: gy: 8 (over z, y), gz: 4 (over x, core).
Axes of the slice: x: 2, y: 2, z: 4, core: 2. Of those that a mesh axis runs over, the one named last changes fastest.
Arguments:
- velocity: float32 [3, 2, 512, 1024], P(None, None, 'gy', 'gz'), may hold values from -6 to 6
Outputs:
- deriv_y: float32 [3, 2, 512, 1024], P(None, None, 'gy', 'gz')
- deriv_z: float32 [3, 2, 512, 1024], P(None, None, 'gy', 'gz')
The draws below stay inside these ranges and needn't reach their ends.
All inputs are finite; a program needn't handle non-finite values.
Results may differ from the reference program's by a relative error of at most 0.00007.
Values sent between devices are 32-bit elements; how exact they have to be, the bound alone decides.
A program may use at most 64 MiB of HBM per device.

```python
import math
import jax
import jax.numpy as jnp
from jax import lax

XW = 2
NY = 512
NZ = 1024


def steps_of(stream_key, shape, cuts, low, top_value):
    def one(dim, blocks):
        steps = jax.random.uniform(jax.random.fold_in(jax.random.fold_in(stream_key, 6), dim), (blocks,), jnp.float32, low / len(cuts), top_value / len(cuts))
        return jnp.repeat(jnp.exp(steps), shape[dim] // blocks).reshape((-1,) + (1,) * (len(shape) - dim - 1))

    loudness = one(*cuts[0])
    for cut in cuts[1:]:
        loudness = loudness * one(*cut)
    return loudness


def normal_values(key, shape, scale, limit, cuts=(), kind=jnp.bfloat16):
    array = scale * jax.random.normal(key, shape, jnp.float32)
    if cuts:
        array = array * steps_of(key, shape, cuts, -0.22, 0.18)
    return jnp.clip(array, -limit, limit).astype(kind)


def setup_inputs(seed: int = 0) -> dict:
    arg_keys = jax.random.split(jax.random.key(seed), 2)
    velocity = normal_values(arg_keys[0], (3, XW, NY, NZ), 1.0, 6.0, ((2, 8), (3, 4)), jnp.float32)
    return {"velocity": velocity}


def derive(plane, axis):
    count = plane.shape[axis]
    spectrum = jnp.fft.rfft(plane, axis=axis)
    wave = 2.0 * math.pi * jnp.arange(count // 2 + 1, dtype=plane.dtype) / count
    factor = (14.0 / 9.0 * jnp.sin(wave) + jnp.sin(2.0 * wave) / 18.0) / (1.0 + 2.0 / 3.0 * jnp.cos(wave))
    if axis == 0:
        factor = factor[:, None]
    result = jnp.fft.irfft(spectrum * (1j * factor), n=count, axis=axis)
    return result.astype(plane.dtype)


def reference(velocity):
    planes = velocity.reshape(3 * XW, NY, NZ)

    def single(plane):
        return derive(plane, 0), derive(plane, 1)

    along_y, along_z = lax.map(single, planes)
    return along_y.reshape(velocity.shape), along_z.reshape(velocity.shape)
```

```python
import functools
import math

import jax
import jax.numpy as jnp
from jax import lax
from jax.experimental import pallas as pl
from jax.experimental.pallas import tpu as pltpu
from jax.sharding import PartitionSpec as P

MESH = pl.DeviceIdType.MESH
ratio = 1.5 - math.sqrt(5.0) / 2.0
near = 7.0 / 9.0
far = 1.0 / 36.0
green = 1.0 / (1.0 - 2.0 / 3.0 * ratio)
tail = green * (near * (1.0 / ratio - ratio) + far * (ratio**2 - 1.0 / ratio**2))
edge = far * green * (ratio - 1.0 / ratio)
log_ratio = math.log(ratio)


def powers(count):
    size = jnp.exp(count.astype(jnp.float32) * log_ratio)
    return jnp.where((count & 1) == 0, size, -size)


def weights(d):
    size = jnp.abs(d)
    value = tail * powers(size) + jnp.where(size == 1, edge, 0.0)
    return jnp.where(d > 0, value, jnp.where(d < 0, -value, 0.0))


def iota(shape, dim):
    return lax.broadcasted_iota(jnp.int32, shape, dim)


def split(x):
    high = x.astype(jnp.bfloat16)
    return high, (x - high.astype(jnp.float32)).astype(jnp.bfloat16)


def dot(a, b, dims=((1,), (0,))):
    return lax.dot_general(a, b, (dims, ((), ())), preferred_element_type=jnp.float32)


def kernel(
    planes, v_hbm, dy_hbm, dz_hbm,
    v, dy, dz, y_out, y_in, z_out, z_in, load_sem, store_sem, send_sem, recv_sem,
):
    rows, nz = v.shape
    ny = rows // planes
    half = y_out.shape[0] // 2
    gy, gz = lax.axis_size("gy"), lax.axis_size("gz")
    iy, iz = lax.axis_index("gy"), lax.axis_index("gz")
    y_next = (lax.rem(iy + 1, gy), iz)
    y_prev = (lax.rem(iy + gy - 1, gy), iz)
    z_next = (iy, lax.rem(iz + 1, gz))
    z_prev = (iy, lax.rem(iz + gz - 1, gz))

    barrier = pltpu.get_barrier_semaphore()
    for other in (y_prev, y_next, z_prev, z_next):
        pl.semaphore_signal(barrier, inc=1, device_id=other, device_id_type=MESH)
    load = pltpu.make_async_copy(v_hbm, v, load_sem)
    load.start()

    place = iota((ny, nz), 0)
    to_next_y = powers(ny - 1 - place)
    to_prev_y = powers(place)
    which, k = iota((16, nz), 0), iota((16, nz), 1)
    message = jnp.where(which == 0, powers(nz - 1 - k), 0.0)
    message = jnp.where((which == 1) & (k == nz - 1), 1.0, message)
    message = jnp.where(which == 8, powers(k), message)
    message = jnp.where((which == 9) & (k == 0), 1.0, message)
    message_hi, message_lo = split(message)
    y_out[...] = jnp.zeros_like(y_out)
    load.wait()

    for p in range(planes):
        plane = v[p * ny:(p + 1) * ny, :]
        y_out[p:p + 1, :] = jnp.sum(plane * to_next_y, axis=0, keepdims=True)
        y_out[planes + p:planes + p + 1, :] = plane[ny - 1:ny, :]
        y_out[half + p:half + p + 1, :] = jnp.sum(plane * to_prev_y, axis=0, keepdims=True)
        y_out[half + planes + p:half + planes + p + 1, :] = plane[0:1, :]
    v_hi, v_lo = split(v[...])
    nt = ((1,), (1,))
    z_out[...] = dot(message_hi, v_hi, nt) + (dot(message_lo, v_hi, nt) + dot(message_hi, v_lo, nt))

    pl.semaphore_wait(barrier, 4)
    copies = []
    for index, (source, target, start, count, other) in enumerate((
        (y_out, y_in, 0, half, y_next),
        (y_out, y_in, half, half, y_prev),
        (z_out, z_in, 0, 8, z_next),
        (z_out, z_in, 8, 8, z_prev),
    )):
        copies.append(pltpu.make_async_remote_copy(
            src_ref=source.at[pl.ds(start, count)],
            dst_ref=target.at[pl.ds(start, count)],
            send_sem=send_sem.at[index],
            recv_sem=recv_sem.at[index],
            device_id=other,
            device_id_type=MESH,
        ))
        copies[-1].start()

    solve_y = weights(iota((ny, ny), 0) - iota((ny, ny), 1))
    y_hi, y_lo = split(solve_y)
    for p in range(planes):
        plane_hi = v_hi[p * ny:(p + 1) * ny, :]
        plane_lo = v_lo[p * ny:(p + 1) * ny, :]
        dy[p * ny:(p + 1) * ny, :] = dot(y_hi, plane_hi) + (dot(y_lo, plane_hi) + dot(y_hi, plane_lo))
    solve_z = weights(iota((nz, nz), 1) - iota((nz, nz), 0))
    z_hi, z_lo = split(solve_z)
    dz[...] = dot(v_hi, z_hi) + (dot(v_lo, z_hi) + dot(v_hi, z_lo))

    spread = jnp.where(which == 0, tail * powers(k + 1), 0.0)
    spread = jnp.where((which == 1) & (k == 0), edge, spread)
    spread = jnp.where(which == 8, -tail * powers(nz - k), spread)
    spread = jnp.where((which == 9) & (k == nz - 1), -edge, spread)
    spread_hi, spread_lo = split(spread)
    from_prev_y = tail * powers(place + 1)
    from_next_y = -tail * powers(ny - place)
    first = jnp.where(iota((8, nz), 0) == 0, edge, 0.0)
    last = jnp.where(iota((8, nz), 0) == 7, -edge, 0.0)

    copies[0].wait_recv()
    copies[1].wait_recv()
    for p in range(planes):
        low, low_edge = y_in[p:p + 1, :], y_in[planes + p:planes + p + 1, :]
        high, high_edge = y_in[half + p:half + p + 1, :], y_in[half + planes + p:half + planes + p + 1, :]
        dy[p * ny:(p + 1) * ny, :] += from_prev_y * low + from_next_y * high
        dy[p * ny:p * ny + 8, :] += first * low_edge
        dy[(p + 1) * ny - 8:(p + 1) * ny, :] += last * high_edge
    store_y = pltpu.make_async_copy(dy, dy_hbm, store_sem.at[0])
    store_y.start()

    copies[2].wait_recv()
    copies[3].wait_recv()
    in_hi, in_lo = split(z_in[...])
    tn = ((0,), (0,))
    dz[...] += dot(in_hi, spread_hi, tn) + (dot(in_lo, spread_hi, tn) + dot(in_hi, spread_lo, tn))
    store_z = pltpu.make_async_copy(dz, dz_hbm, store_sem.at[1])
    store_z.start()
    for copy in copies:
        copy.wait_send()
    store_y.wait()
    store_z.wait()


def per_device(velocity):
    planes = velocity.shape[0] * velocity.shape[1]
    ny, nz = velocity.shape[2:]
    flat = jax.ShapeDtypeStruct((planes * ny, nz), jnp.float32)
    half = (2 * planes + 7) // 8 * 8
    block = pltpu.VMEM(flat.shape, jnp.float32)
    deriv_y, deriv_z = pl.pallas_call(
        functools.partial(kernel, planes),
        out_shape=(flat, flat),
        in_specs=[pl.BlockSpec(memory_space=pl.ANY)],
        out_specs=(pl.BlockSpec(memory_space=pl.ANY),) * 2,
        scratch_shapes=[
            block, block, block,
            pltpu.VMEM((2 * half, nz), jnp.float32),
            pltpu.VMEM((2 * half, nz), jnp.float32),
            pltpu.VMEM((16, planes * ny), jnp.float32),
            pltpu.VMEM((16, planes * ny), jnp.float32),
            pltpu.SemaphoreType.DMA,
            pltpu.SemaphoreType.DMA((2,)),
            pltpu.SemaphoreType.DMA((4,)),
            pltpu.SemaphoreType.DMA((4,)),
        ],
        compiler_params=pltpu.CompilerParams(
            collective_id=0, has_side_effects=True, vmem_limit_bytes=16 * 2**20
        ),
        cost_estimate=pl.CostEstimate(
            flops=6 * planes * ny * nz * (ny + nz), bytes_accessed=12 * planes * ny * nz, transcendentals=0
        ),
    )(velocity.reshape(flat.shape))
    return deriv_y.reshape(velocity.shape), deriv_z.reshape(velocity.shape)


def solution(mesh):
    spec = P(None, None, "gy", "gz")
    return jax.shard_map(
        per_device, mesh=mesh, in_specs=(spec,), out_specs=(spec, spec), check_vma=False
    )
```

```python
import functools
import math

import jax
import jax.numpy as jnp
from jax import lax
from jax.experimental import pallas as pl
from jax.experimental.pallas import tpu as pltpu
from jax.sharding import PartitionSpec as P

MESH = pl.DeviceIdType.MESH
ratio = 1.5 - math.sqrt(5.0) / 2.0
near = 7.0 / 9.0
far = 1.0 / 36.0
green = 1.0 / (1.0 - 2.0 / 3.0 * ratio)
tail = green * (near * (1.0 / ratio - ratio) + far * (ratio**2 - 1.0 / ratio**2))
edge = far * green * (ratio - 1.0 / ratio)
log_ratio = math.log(ratio)


def powers(count):
    size = jnp.exp(count.astype(jnp.float32) * log_ratio)
    return jnp.where((count & 1) == 0, size, -size)


def weights(d):
    size = jnp.abs(d)
    value = tail * powers(size) + jnp.where(size == 1, edge, 0.0)
    return jnp.where(d > 0, value, jnp.where(d < 0, -value, 0.0))


def iota(shape, dim):
    return lax.broadcasted_iota(jnp.int32, shape, dim)


def split(x):
    high = x.astype(jnp.bfloat16)
    return high, (x - high.astype(jnp.float32)).astype(jnp.bfloat16)


def dot(a, b, dims=((1,), (0,))):
    return lax.dot_general(a, b, (dims, ((), ())), preferred_element_type=jnp.float32)


def kernel(planes, v_hbm, dy, dz, v, y_out, y_in, z_out, z_in, load_sem, send_sem, recv_sem):
    rows, nz = v.shape
    ny = rows // planes
    half = y_out.shape[0] // 2
    gy, gz = lax.axis_size("gy"), lax.axis_size("gz")
    iy, iz = lax.axis_index("gy"), lax.axis_index("gz")
    y_next = (lax.rem(iy + 1, gy), iz)
    y_prev = (lax.rem(iy + gy - 1, gy), iz)
    z_next = (iy, lax.rem(iz + 1, gz))
    z_prev = (iy, lax.rem(iz + gz - 1, gz))

    barrier = pltpu.get_barrier_semaphore()
    for other in (y_prev, y_next, z_prev, z_next):
        pl.semaphore_signal(barrier, inc=1, device_id=other, device_id_type=MESH)
    loads = []
    for p in range(planes):
        part = pl.ds(p * ny, ny)
        loads.append(pltpu.make_async_copy(v_hbm.at[part], v.at[part], load_sem.at[p]))
        loads[-1].start()

    place = iota((ny, nz), 0)
    to_next_y = powers(ny - 1 - place)
    to_prev_y = powers(place)
    which, k = iota((16, nz), 0), iota((16, nz), 1)
    message = jnp.where(which == 0, powers(nz - 1 - k), 0.0)
    message = jnp.where((which == 1) & (k == nz - 1), 1.0, message)
    message = jnp.where(which == 8, powers(k), message)
    message = jnp.where((which == 9) & (k == 0), 1.0, message)
    message_hi, message_lo = split(message)
    y_out[...] = jnp.zeros_like(y_out)
    y_hi, y_lo = split(weights(iota((ny, ny), 0) - iota((ny, ny), 1)))
    z_hi, z_lo = split(weights(iota((nz, nz), 1) - iota((nz, nz), 0)))
    spread = jnp.where(which == 0, tail * powers(k + 1), 0.0)
    spread = jnp.where((which == 1) & (k == 0), edge, spread)
    spread = jnp.where(which == 8, -tail * powers(nz - k), spread)
    spread = jnp.where((which == 9) & (k == nz - 1), -edge, spread)
    spread_hi, spread_lo = split(spread)
    from_prev_y = tail * powers(place + 1)
    from_next_y = -tail * powers(ny - place)
    first = jnp.where(iota((8, nz), 0) == 0, edge, 0.0)
    last = jnp.where(iota((8, nz), 0) == 7, -edge, 0.0)

    for p in range(planes):
        loads[p].wait()
        plane = v[p * ny:(p + 1) * ny, :]
        y_out[p:p + 1, :] = jnp.sum(plane * to_next_y, axis=0, keepdims=True)
        y_out[planes + p:planes + p + 1, :] = plane[ny - 1:ny, :]
        y_out[half + p:half + p + 1, :] = jnp.sum(plane * to_prev_y, axis=0, keepdims=True)
        y_out[half + planes + p:half + planes + p + 1, :] = plane[0:1, :]
    v_hi, v_lo = split(v[...])
    nt = ((1,), (1,))
    z_out[...] = dot(message_hi, v_hi, nt) + (dot(message_lo, v_hi, nt) + dot(message_hi, v_lo, nt))

    pl.semaphore_wait(barrier, 4)
    copies = []
    for index, (source, target, start, count, other) in enumerate((
        (y_out, y_in, 0, half, y_next),
        (y_out, y_in, half, half, y_prev),
        (z_out, z_in, 0, 8, z_next),
        (z_out, z_in, 8, 8, z_prev),
    )):
        copies.append(pltpu.make_async_remote_copy(
            src_ref=source.at[pl.ds(start, count)],
            dst_ref=target.at[pl.ds(start, count)],
            send_sem=send_sem.at[index],
            recv_sem=recv_sem.at[index],
            device_id=other,
            device_id_type=MESH,
        ))
        copies[-1].start()

    for p in range(planes):
        plane_hi = v_hi[p * ny:(p + 1) * ny, :]
        plane_lo = v_lo[p * ny:(p + 1) * ny, :]
        dy[p * ny:(p + 1) * ny, :] = dot(y_hi, plane_hi) + (dot(y_lo, plane_hi) + dot(y_hi, plane_lo))
    dz[...] = dot(v_hi, z_hi) + (dot(v_lo, z_hi) + dot(v_hi, z_lo))

    copies[2].wait_recv()
    copies[3].wait_recv()
    in_hi, in_lo = split(z_in[...])
    tn = ((0,), (0,))
    dz[...] += dot(in_hi, spread_hi, tn) + (dot(in_lo, spread_hi, tn) + dot(in_hi, spread_lo, tn))

    copies[0].wait_recv()
    copies[1].wait_recv()
    for p in range(planes):
        low, low_edge = y_in[p:p + 1, :], y_in[planes + p:planes + p + 1, :]
        high, high_edge = y_in[half + p:half + p + 1, :], y_in[half + planes + p:half + planes + p + 1, :]
        dy[p * ny:(p + 1) * ny, :] += from_prev_y * low + from_next_y * high
        dy[p * ny:p * ny + 8, :] += first * low_edge
        dy[(p + 1) * ny - 8:(p + 1) * ny, :] += last * high_edge
    for copy in copies:
        copy.wait_send()


def store(dy, dz, dy_hbm, dz_hbm, sem):
    copies = (
        pltpu.make_async_copy(dy, dy_hbm, sem.at[0]),
        pltpu.make_async_copy(dz, dz_hbm, sem.at[1]),
    )
    for copy in copies:
        copy.start()
    for copy in copies:
        copy.wait()


def per_device(velocity):
    planes = velocity.shape[0] * velocity.shape[1]
    ny, nz = velocity.shape[2:]
    flat = (planes * ny, nz)
    half = (2 * planes + 7) // 8 * 8
    in_vmem = pl.BlockSpec(memory_space=pltpu.VMEM)
    in_hbm = pl.BlockSpec(memory_space=pltpu.HBM)
    result = pltpu.VMEM(flat, jnp.float32)
    parts = pl.pallas_call(
        functools.partial(kernel, planes),
        out_shape=(result, result),
        in_specs=[in_hbm],
        out_specs=(in_vmem, in_vmem),
        scratch_shapes=[
            pltpu.VMEM(flat, jnp.float32),
            pltpu.VMEM((2 * half, nz), jnp.float32),
            pltpu.VMEM((2 * half, nz), jnp.float32),
            pltpu.VMEM((16, planes * ny), jnp.float32),
            pltpu.VMEM((16, planes * ny), jnp.float32),
            pltpu.SemaphoreType.DMA((planes,)),
            pltpu.SemaphoreType.DMA((4,)),
            pltpu.SemaphoreType.DMA((4,)),
        ],
        compiler_params=pltpu.CompilerParams(
            collective_id=0, has_side_effects=True, vmem_limit_bytes=16 * 2**20
        ),
    )(pltpu.with_memory_space_constraint(velocity.reshape(flat), pltpu.HBM))
    stored = pltpu.HBM(flat, jnp.float32)
    deriv_y, deriv_z = pl.pallas_call(
        store,
        out_shape=(stored, stored),
        in_specs=[in_vmem, in_vmem],
        out_specs=(in_hbm, in_hbm),
        scratch_shapes=[pltpu.SemaphoreType.DMA((2,))],
        compiler_params=pltpu.CompilerParams(vmem_limit_bytes=4 * 2**20),
    )(*(pltpu.with_memory_space_constraint(part, pltpu.VMEM) for part in parts))
    return deriv_y.reshape(velocity.shape), deriv_z.reshape(velocity.shape)


def solution(mesh):
    spec = P(None, None, "gy", "gz")
    return jax.shard_map(
        per_device, mesh=mesh, in_specs=(spec,), out_specs=(spec, spec), check_vma=False
    )
```

```python
import functools
import math

import jax
import jax.numpy as jnp
from jax import lax
from jax.experimental import pallas as pl
from jax.experimental.pallas import tpu as pltpu
from jax.sharding import PartitionSpec as P

MESH = pl.DeviceIdType.MESH
ratio = 1.5 - math.sqrt(5.0) / 2.0
near = 7.0 / 9.0
far = 1.0 / 36.0
green = 1.0 / (1.0 - 2.0 / 3.0 * ratio)
tail = green * (near * (1.0 / ratio - ratio) + far * (ratio**2 - 1.0 / ratio**2))
edge = far * green * (ratio - 1.0 / ratio)
log_ratio = math.log(ratio)


def powers(count):
    size = jnp.exp(count.astype(jnp.float32) * log_ratio)
    return jnp.where((count & 1) == 0, size, -size)


def weights(d):
    size = jnp.abs(d)
    value = tail * powers(size) + jnp.where(size == 1, edge, 0.0)
    return jnp.where(d > 0, value, jnp.where(d < 0, -value, 0.0))


def iota(shape, dim):
    return lax.broadcasted_iota(jnp.int32, shape, dim)


def split(x):
    high = x.astype(jnp.bfloat16)
    return high, (x - high.astype(jnp.float32)).astype(jnp.bfloat16)


def dot(a, b, dims=((1,), (0,))):
    return lax.dot_general(a, b, (dims, ((), ())), preferred_element_type=jnp.float32)


def exchange(planes, v_hbm, dy, dz, y_in, z_in, v, y_out, z_out, load_sem, send_sem, recv_sem):
    rows, nz = v.shape
    ny = rows // planes
    half = y_out.shape[0] // 2
    gy, gz = lax.axis_size("gy"), lax.axis_size("gz")
    iy, iz = lax.axis_index("gy"), lax.axis_index("gz")
    y_next = (lax.rem(iy + 1, gy), iz)
    y_prev = (lax.rem(iy + gy - 1, gy), iz)
    z_next = (iy, lax.rem(iz + 1, gz))
    z_prev = (iy, lax.rem(iz + gz - 1, gz))

    barrier = pltpu.get_barrier_semaphore()
    for other in (y_prev, y_next, z_prev, z_next):
        pl.semaphore_signal(barrier, inc=1, device_id=other, device_id_type=MESH)
    loads = []
    for p in range(planes):
        part = pl.ds(p * ny, ny)
        loads.append(pltpu.make_async_copy(v_hbm.at[part], v.at[part], load_sem.at[p]))
        loads[-1].start()

    def send(index, source, target, start, count, other):
        copy = pltpu.make_async_remote_copy(
            src_ref=source.at[pl.ds(start, count)],
            dst_ref=target.at[pl.ds(start, count)],
            send_sem=send_sem.at[index],
            recv_sem=recv_sem.at[index],
            device_id=other,
            device_id_type=MESH,
        )
        copy.start()
        return copy

    place = iota((ny, nz), 0)
    to_next_y = powers(ny - 1 - place)
    to_prev_y = powers(place)
    which, k = iota((16, nz), 0), iota((16, nz), 1)
    message = jnp.where(which == 0, powers(nz - 1 - k), 0.0)
    message = jnp.where((which == 1) & (k == nz - 1), 1.0, message)
    message = jnp.where(which == 8, powers(k), message)
    message = jnp.where((which == 9) & (k == 0), 1.0, message)
    message_hi, message_lo = split(message)
    message_both = jnp.concatenate([message_hi, message_lo], axis=0)
    y_out[...] = jnp.zeros_like(y_out)
    y_hi, y_lo = split(weights(iota((ny, ny), 0) - iota((ny, ny), 1)))
    z_hi, z_lo = split(weights(iota((nz, nz), 1) - iota((nz, nz), 0)))

    for p in range(planes):
        loads[p].wait()
        plane = v[p * ny:(p + 1) * ny, :]
        y_out[p:p + 1, :] = jnp.sum(plane * to_next_y, axis=0, keepdims=True)
        y_out[planes + p:planes + p + 1, :] = plane[ny - 1:ny, :]
        y_out[half + p:half + p + 1, :] = jnp.sum(plane * to_prev_y, axis=0, keepdims=True)
        y_out[half + planes + p:half + planes + p + 1, :] = plane[0:1, :]
    pl.semaphore_wait(barrier, 4)
    copies = [
        send(0, y_out, y_in, 0, half, y_next),
        send(1, y_out, y_in, half, half, y_prev),
    ]
    v_hi, v_lo = split(v[...])
    nt = ((1,), (1,))
    both = dot(message_both, v_hi, nt)
    z_out[...] = both[:16] + (both[16:] + dot(message_hi, v_lo, nt))
    copies.append(send(2, z_out, z_in, 0, 8, z_next))
    copies.append(send(3, z_out, z_in, 8, 8, z_prev))

    for p in range(planes):
        plane_hi = v_hi[p * ny:(p + 1) * ny, :]
        plane_lo = v_lo[p * ny:(p + 1) * ny, :]
        dy[p * ny:(p + 1) * ny, :] = dot(y_hi, plane_hi) + (dot(y_lo, plane_hi) + dot(y_hi, plane_lo))
    dz[...] = dot(v_hi, z_hi) + (dot(v_lo, z_hi) + dot(v_hi, z_lo))

    for copy in copies:
        copy.wait()


def finish(planes, own_y, own_z, y_in, z_in, dy_hbm, dz_hbm, dy, dz, y_sem, z_sem):
    rows, nz = own_z.shape
    ny = rows // planes
    half = y_in.shape[0] // 2
    which, k = iota((16, nz), 0), iota((16, nz), 1)
    spread = jnp.where(which == 0, tail * powers(k + 1), 0.0)
    spread = jnp.where((which == 1) & (k == 0), edge, spread)
    spread = jnp.where(which == 8, -tail * powers(nz - k), spread)
    spread = jnp.where((which == 9) & (k == nz - 1), -edge, spread)
    spread_hi, spread_lo = split(spread)
    in_hi, in_lo = split(z_in[...])
    z_part = dot(
        jnp.concatenate([in_hi, in_lo, in_hi], axis=0),
        jnp.concatenate([spread_hi, spread_hi, spread_lo], axis=0),
        ((0,), (0,)),
    )
    place = iota((ny, nz), 0)
    from_prev_y = tail * powers(place + 1)
    from_next_y = -tail * powers(ny - place)
    first = jnp.where(place == 0, edge, 0.0)
    last = jnp.where(place == ny - 1, -edge, 0.0)
    copies = []

    def store(source, target, p, sem):
        part = pl.ds(p * ny, ny)
        copies.append(pltpu.make_async_copy(source.at[part], target.at[part], sem.at[p]))
        copies[-1].start()

    for p in range(planes):
        low, low_edge = y_in[p:p + 1, :], y_in[planes + p:planes + p + 1, :]
        high, high_edge = y_in[half + p:half + p + 1, :], y_in[half + planes + p:half + planes + p + 1, :]
        part = slice(p * ny, (p + 1) * ny)
        dy[part, :] = (own_y[part, :] + (from_prev_y * low + from_next_y * high)) + (first * low_edge + last * high_edge)
        store(dy, dy_hbm, p, y_sem)
    for p in range(planes):
        part = slice(p * ny, (p + 1) * ny)
        dz[part, :] = own_z[part, :] + z_part[part, :]
        store(dz, dz_hbm, p, z_sem)
    for copy in copies:
        copy.wait()


def per_device(velocity):
    planes = velocity.shape[0] * velocity.shape[1]
    ny, nz = velocity.shape[2:]
    flat = (planes * ny, nz)
    half = (2 * planes + 7) // 8 * 8
    block = pltpu.VMEM(flat, jnp.float32)
    y_message = pltpu.VMEM((2 * half, nz), jnp.float32)
    z_message = pltpu.VMEM((16, planes * ny), jnp.float32)
    in_vmem = pl.BlockSpec(memory_space=pltpu.VMEM)
    in_hbm = pl.BlockSpec(memory_space=pltpu.HBM)
    parts = pl.pallas_call(
        functools.partial(exchange, planes),
        out_shape=(block, block, y_message, z_message),
        in_specs=[in_hbm],
        out_specs=(in_vmem,) * 4,
        scratch_shapes=[
            block, y_message, z_message,
            pltpu.SemaphoreType.DMA((planes,)),
            pltpu.SemaphoreType.DMA((4,)),
            pltpu.SemaphoreType.DMA((4,)),
        ],
        compiler_params=pltpu.CompilerParams(
            collective_id=0, has_side_effects=True, vmem_limit_bytes=16 * 2**20
        ),
    )(pltpu.with_memory_space_constraint(velocity.reshape(flat), pltpu.HBM))
    stored = pltpu.HBM(flat, jnp.float32)
    deriv_y, deriv_z = pl.pallas_call(
        functools.partial(finish, planes),
        out_shape=(stored, stored),
        in_specs=[in_vmem] * 4,
        out_specs=(in_hbm, in_hbm),
        scratch_shapes=[
            block, block,
            pltpu.SemaphoreType.DMA((planes,)),
            pltpu.SemaphoreType.DMA((planes,)),
        ],
        compiler_params=pltpu.CompilerParams(vmem_limit_bytes=16 * 2**20),
    )(*(pltpu.with_memory_space_constraint(part, pltpu.VMEM) for part in parts))
    return deriv_y.reshape(velocity.shape), deriv_z.reshape(velocity.shape)


def solution(mesh):
    spec = P(None, None, "gy", "gz")
    return jax.shard_map(
        per_device, mesh=mesh, in_specs=(spec,), out_specs=(spec, spec), check_vma=False
    )
```

```python
import functools
import math

import jax
import jax.numpy as jnp
from jax import lax
from jax.experimental import pallas as pl
from jax.experimental.pallas import tpu as pltpu
from jax.sharding import PartitionSpec as P

MESH = pl.DeviceIdType.MESH
ratio = 1.5 - math.sqrt(5.0) / 2.0
near = 7.0 / 9.0
far = 1.0 / 36.0
green = 1.0 / (1.0 - 2.0 / 3.0 * ratio)
tail = green * (near * (1.0 / ratio - ratio) + far * (ratio**2 - 1.0 / ratio**2))
edge = far * green * (ratio - 1.0 / ratio)
log_ratio = math.log(ratio)


def powers(count):
    size = jnp.exp(count.astype(jnp.float32) * log_ratio)
    return jnp.where((count & 1) == 0, size, -size)


def weights(d):
    size = jnp.abs(d)
    value = tail * powers(size) + jnp.where(size == 1, edge, 0.0)
    return jnp.where(d > 0, value, jnp.where(d < 0, -value, 0.0))


def iota(shape, dim):
    return lax.broadcasted_iota(jnp.int32, shape, dim)


def split(x):
    high = x.astype(jnp.bfloat16)
    return high, (x - high.astype(jnp.float32)).astype(jnp.bfloat16)


def dot(a, b, dims=((1,), (0,))):
    return lax.dot_general(a, b, (dims, ((), ())), preferred_element_type=jnp.float32)


def put_row(ref, start, planes, p, row):
    for c in range(row.shape[1] // 128):
        place = start + c * planes + p
        ref[place:place + 1, :] = row[:, c * 128:(c + 1) * 128]


def get_row(ref, start, planes, p, nz):
    places = [start + c * planes + p for c in range(nz // 128)]
    return jnp.concatenate([ref[place:place + 1, :] for place in places], axis=1)


def exchange(planes, v_hbm, dy, dz, y_in, y_weight, v, y_out, z_out, z_in, load_sem, send_sem, recv_sem):
    rows, nz = v.shape
    ny = rows // planes
    half = y_out.shape[0] // 2
    gy, gz = lax.axis_size("gy"), lax.axis_size("gz")
    iy, iz = lax.axis_index("gy"), lax.axis_index("gz")
    y_next = (lax.rem(iy + 1, gy), iz)
    y_prev = (lax.rem(iy + gy - 1, gy), iz)
    z_next = (iy, lax.rem(iz + 1, gz))
    z_prev = (iy, lax.rem(iz + gz - 1, gz))

    barrier = pltpu.get_barrier_semaphore()
    for other in (y_prev, y_next, z_prev, z_next):
        pl.semaphore_signal(barrier, inc=1, device_id=other, device_id_type=MESH)
    loads = []
    for p in range(planes):
        part = pl.ds(p * ny, ny)
        loads.append(pltpu.make_async_copy(v_hbm.at[part], v.at[part], load_sem.at[p]))
        loads[-1].start()

    def send(index, source, target, start, count, other):
        copy = pltpu.make_async_remote_copy(
            src_ref=source.at[pl.ds(start, count)],
            dst_ref=target.at[pl.ds(start, count)],
            send_sem=send_sem.at[index],
            recv_sem=recv_sem.at[index],
            device_id=other,
            device_id_type=MESH,
        )
        copy.start()
        return copy

    place = iota((ny, nz), 0)
    to_next_y = powers(ny - 1 - place)
    to_prev_y = powers(place)
    which, k = iota((16, nz), 0), iota((16, nz), 1)
    message = jnp.where(which == 0, powers(nz - 1 - k), 0.0)
    message = jnp.where((which == 1) & (k == nz - 1), 1.0, message)
    message = jnp.where(which == 8, powers(k), message)
    message = jnp.where((which == 9) & (k == 0), 1.0, message)
    message_hi, message_lo = split(message)
    message_both = jnp.concatenate([message_hi, message_lo], axis=0)
    y_hi, y_lo = split(weights(iota((ny, ny), 0) - iota((ny, ny), 1)))
    z_hi, z_lo = split(weights(iota((nz, nz), 1) - iota((nz, nz), 0)))

    spread = jnp.where(which == 0, tail * powers(k + 1), 0.0)
    spread = jnp.where((which == 1) & (k == 0), edge, spread)
    spread = jnp.where(which == 8, -tail * powers(nz - k), spread)
    spread = jnp.where((which == 9) & (k == nz - 1), -edge, spread)
    spread_hi, spread_lo = split(spread)
    if half > 2 * planes * (nz // 128):
        y_out[...] = jnp.zeros_like(y_out)
    y_weight[:ny, :] = tail * powers(place + 1)
    y_weight[ny:, :] = -tail * powers(ny - place)

    for p in range(planes):
        loads[p].wait()
        plane = v[p * ny:(p + 1) * ny, :]
        put_row(y_out, 0, planes, p, jnp.sum(plane * to_next_y, axis=0, keepdims=True))
        put_row(y_out, nz // 128 * planes, planes, p, plane[ny - 1:ny, :])
        put_row(y_out, half, planes, p, jnp.sum(plane * to_prev_y, axis=0, keepdims=True))
        put_row(y_out, half + nz // 128 * planes, planes, p, plane[0:1, :])
    pl.semaphore_wait(barrier, 4)
    copies = [
        send(0, y_out, y_in, 0, half, y_next),
        send(1, y_out, y_in, half, half, y_prev),
    ]
    v_hi, v_lo = split(v[...])
    nt = ((1,), (1,))
    both = dot(message_both, v_hi, nt)
    z_out[...] = both[:16] + (both[16:] + dot(message_hi, v_lo, nt))
    copies.append(send(2, z_out, z_in, 0, 8, z_next))
    copies.append(send(3, z_out, z_in, 8, 8, z_prev))

    for p in range(planes):
        plane_hi = v_hi[p * ny:(p + 1) * ny, :]
        plane_lo = v_lo[p * ny:(p + 1) * ny, :]
        dy[p * ny:(p + 1) * ny, :] = dot(y_hi, plane_hi) + (dot(y_lo, plane_hi) + dot(y_hi, plane_lo))
    dz[...] = dot(v_hi, z_hi) + (dot(v_lo, z_hi) + dot(v_hi, z_lo))

    copies[2].wait_recv()
    copies[3].wait_recv()
    in_hi, in_lo = split(z_in[...])
    dz[...] += dot(
        jnp.concatenate([in_hi, in_lo, in_hi], axis=0),
        jnp.concatenate([spread_hi, spread_hi, spread_lo], axis=0),
        ((0,), (0,)),
    )
    copies[0].wait_recv()
    copies[1].wait_recv()
    for copy in copies:
        copy.wait_send()


def finish(planes, own_y, dz, y_in, y_weight, dy_hbm, dz_hbm, dy, y_sem, z_sem):
    rows, nz = own_y.shape
    ny = rows // planes
    half = y_in.shape[0] // 2
    copies = []

    def store(source, target, p, sem):
        part = pl.ds(p * ny, ny)
        copies.append(pltpu.make_async_copy(source.at[part], target.at[part], sem.at[p]))
        copies[-1].start()

    for p in range(planes):
        store(dz, dz_hbm, p, z_sem)
    from_prev_y, from_next_y = y_weight[:ny, :], y_weight[ny:, :]
    first = jnp.where(iota((8, nz), 0) == 0, edge, 0.0)
    last = jnp.where(iota((8, nz), 0) == 7, -edge, 0.0)
    for p in range(planes):
        low = get_row(y_in, 0, planes, p, nz)
        low_edge = get_row(y_in, nz // 128 * planes, planes, p, nz)
        high = get_row(y_in, half, planes, p, nz)
        high_edge = get_row(y_in, half + nz // 128 * planes, planes, p, nz)
        part = slice(p * ny, (p + 1) * ny)
        dy[part, :] = own_y[part, :] + (from_prev_y * low + from_next_y * high)
        dy[p * ny:p * ny + 8, :] += first * low_edge
        dy[(p + 1) * ny - 8:(p + 1) * ny, :] += last * high_edge
        store(dy, dy_hbm, p, y_sem)
    for copy in copies:
        copy.wait()


def per_device(velocity):
    planes = velocity.shape[0] * velocity.shape[1]
    ny, nz = velocity.shape[2:]
    flat = (planes * ny, nz)
    half = (2 * planes * (nz // 128) + 7) // 8 * 8
    block = pltpu.VMEM(flat, jnp.float32)
    y_message = pltpu.VMEM((2 * half, 128), jnp.float32)
    z_message = pltpu.VMEM((16, planes * ny), jnp.float32)
    in_vmem = pl.BlockSpec(memory_space=pltpu.VMEM)
    in_hbm = pl.BlockSpec(memory_space=pltpu.HBM)
    parts = pl.pallas_call(
        functools.partial(exchange, planes),
        out_shape=(block, block, y_message, pltpu.VMEM((2 * ny, nz), jnp.float32)),
        in_specs=[in_hbm],
        out_specs=(in_vmem,) * 4,
        scratch_shapes=[
            block, y_message, z_message, z_message,
            pltpu.SemaphoreType.DMA((planes,)),
            pltpu.SemaphoreType.DMA((4,)),
            pltpu.SemaphoreType.DMA((4,)),
        ],
        compiler_params=pltpu.CompilerParams(
            collective_id=0, has_side_effects=True, vmem_limit_bytes=16 * 2**20
        ),
    )(pltpu.with_memory_space_constraint(velocity.reshape(flat), pltpu.HBM))
    stored = pltpu.HBM(flat, jnp.float32)
    deriv_y, deriv_z = pl.pallas_call(
        functools.partial(finish, planes),
        out_shape=(stored, stored),
        in_specs=[in_vmem] * 4,
        out_specs=(in_hbm, in_hbm),
        scratch_shapes=[
            block,
            pltpu.SemaphoreType.DMA((planes,)),
            pltpu.SemaphoreType.DMA((planes,)),
        ],
        compiler_params=pltpu.CompilerParams(vmem_limit_bytes=16 * 2**20),
    )(*(pltpu.with_memory_space_constraint(part, pltpu.VMEM) for part in parts))
    return deriv_y.reshape(velocity.shape), deriv_z.reshape(velocity.shape)


def solution(mesh):
    spec = P(None, None, "gy", "gz")
    return jax.shard_map(
        per_device, mesh=mesh, in_specs=(spec,), out_specs=(spec, spec), check_vma=False
    )
```

```python
import functools
import math

import jax
import jax.numpy as jnp
from jax import lax
from jax.experimental import pallas as pl
from jax.experimental.pallas import tpu as pltpu
from jax.sharding import PartitionSpec as P

MESH = pl.DeviceIdType.MESH
ratio = 1.5 - math.sqrt(5.0) / 2.0
near = 7.0 / 9.0
far = 1.0 / 36.0
green = 1.0 / (1.0 - 2.0 / 3.0 * ratio)
tail = green * (near * (1.0 / ratio - ratio) + far * (ratio**2 - 1.0 / ratio**2))
edge = far * green * (ratio - 1.0 / ratio)
log_ratio = math.log(ratio)


def powers(count):
    size = jnp.exp(count.astype(jnp.float32) * log_ratio)
    return jnp.where((count & 1) == 0, size, -size)


def weights(d):
    size = jnp.abs(d)
    value = tail * powers(size) + jnp.where(size == 1, edge, 0.0)
    return jnp.where(d > 0, value, jnp.where(d < 0, -value, 0.0))


def iota(shape, dim):
    return lax.broadcasted_iota(jnp.int32, shape, dim)


def split(x):
    high = x.astype(jnp.bfloat16)
    return high, (x - high.astype(jnp.float32)).astype(jnp.bfloat16)


def dot(a, b, dims=((1,), (0,))):
    return lax.dot_general(a, b, (dims, ((), ())), preferred_element_type=jnp.float32)


def put_row(ref, start, planes, p, row):
    for c in range(row.shape[1] // 128):
        place = start + c * planes + p
        ref[place:place + 1, :] = row[:, c * 128:(c + 1) * 128]


def get_row(ref, start, planes, p, nz):
    places = [start + c * planes + p for c in range(nz // 128)]
    return jnp.concatenate([ref[place:place + 1, :] for place in places], axis=1)


def exchange(planes, v_hbm, dy, dz, y_in, y_weight, v, y_out, z_out, z_in, load_sem, send_sem, recv_sem):
    rows, nz = v.shape
    ny = rows // planes
    half = y_out.shape[0] // 2
    gy, gz = lax.axis_size("gy"), lax.axis_size("gz")
    iy, iz = lax.axis_index("gy"), lax.axis_index("gz")
    y_next = (lax.rem(iy + 1, gy), iz)
    y_prev = (lax.rem(iy + gy - 1, gy), iz)
    z_next = (iy, lax.rem(iz + 1, gz))
    z_prev = (iy, lax.rem(iz + gz - 1, gz))

    barrier = pltpu.get_barrier_semaphore()
    for other in (y_prev, y_next, z_prev, z_next):
        pl.semaphore_signal(barrier, inc=1, device_id=other, device_id_type=MESH)
    loads = []
    for p in range(planes):
        part = pl.ds(p * ny, ny)
        loads.append(pltpu.make_async_copy(v_hbm.at[part], v.at[part], load_sem.at[p]))
        loads[-1].start()

    def send(index, source, target, start, count, other):
        copy = pltpu.make_async_remote_copy(
            src_ref=source.at[pl.ds(start, count)],
            dst_ref=target.at[pl.ds(start, count)],
            send_sem=send_sem.at[index],
            recv_sem=recv_sem.at[index],
            device_id=other,
            device_id_type=MESH,
        )
        copy.start()
        return copy

    place = iota((ny, 128), 0)
    to_next_y = jnp.concatenate([powers(ny - 1 - place)] * (nz // 128), axis=1)
    to_prev_y = jnp.concatenate([powers(place)] * (nz // 128), axis=1)
    which, k = iota((16, nz), 0), iota((16, nz), 1)
    message = jnp.where(which == 0, powers(nz - 1 - k), 0.0)
    message = jnp.where((which == 1) & (k == nz - 1), 1.0, message)
    message = jnp.where(which == 8, powers(k), message)
    message = jnp.where((which == 9) & (k == 0), 1.0, message)
    message_hi, message_lo = split(message)
    message_both = jnp.concatenate([message_hi, message_lo], axis=0)
    y_hi, y_lo = split(weights(iota((ny, ny), 0) - iota((ny, ny), 1)))
    z_hi, z_lo = split(weights(iota((nz, nz), 1) - iota((nz, nz), 0)))

    spread = jnp.where(which == 0, tail * powers(k + 1), 0.0)
    spread = jnp.where((which == 1) & (k == 0), edge, spread)
    spread = jnp.where(which == 8, -tail * powers(nz - k), spread)
    spread = jnp.where((which == 9) & (k == nz - 1), -edge, spread)
    spread_hi, spread_lo = split(spread)
    if half > 2 * planes * (nz // 128):
        y_out[...] = jnp.zeros_like(y_out)
    y_weight[:ny, :] = -tail * ratio * to_prev_y
    y_weight[ny:, :] = tail * ratio * to_next_y

    for p in range(planes):
        loads[p].wait()
        plane = v[p * ny:(p + 1) * ny, :]
        put_row(y_out, 0, planes, p, jnp.sum(plane * to_next_y, axis=0, keepdims=True))
        put_row(y_out, nz // 128 * planes, planes, p, plane[ny - 1:ny, :])
        put_row(y_out, half, planes, p, jnp.sum(plane * to_prev_y, axis=0, keepdims=True))
        put_row(y_out, half + nz // 128 * planes, planes, p, plane[0:1, :])
    v_hi, v_lo = split(v[...])
    nt = ((1,), (1,))
    both = dot(message_both, v_hi, nt)
    z_out[...] = both[:16] + (both[16:] + dot(message_hi, v_lo, nt))
    pl.semaphore_wait(barrier, 4)
    copies = [
        send(0, y_out, y_in, 0, half, y_next),
        send(1, y_out, y_in, half, half, y_prev),
    ]
    copies.append(send(2, z_out, z_in, 0, 8, z_next))
    copies.append(send(3, z_out, z_in, 8, 8, z_prev))

    for p in range(planes):
        plane_hi = v_hi[p * ny:(p + 1) * ny, :]
        plane_lo = v_lo[p * ny:(p + 1) * ny, :]
        dy[p * ny:(p + 1) * ny, :] = dot(y_hi, plane_hi) + (dot(y_lo, plane_hi) + dot(y_hi, plane_lo))
    dz[...] = dot(v_hi, z_hi) + (dot(v_lo, z_hi) + dot(v_hi, z_lo))

    copies[2].wait_recv()
    copies[3].wait_recv()
    in_hi, in_lo = split(z_in[...])
    dz[...] += dot(
        jnp.concatenate([in_hi, in_lo, in_hi], axis=0),
        jnp.concatenate([spread_hi, spread_hi, spread_lo], axis=0),
        ((0,), (0,)),
    )
    copies[0].wait_recv()
    copies[1].wait_recv()
    for copy in copies:
        copy.wait_send()


def finish(planes, own_y, dz, y_in, y_weight, dy_hbm, dz_hbm, dy, y_sem, z_sem):
    rows, nz = own_y.shape
    ny = rows // planes
    half = y_in.shape[0] // 2
    copies = []

    def store(source, target, p, sem):
        part = pl.ds(p * ny, ny)
        copies.append(pltpu.make_async_copy(source.at[part], target.at[part], sem.at[p]))
        copies[-1].start()

    for p in range(planes):
        store(dz, dz_hbm, p, z_sem)
    from_prev_y, from_next_y = y_weight[:ny, :], y_weight[ny:, :]
    first = jnp.where(iota((8, nz), 0) == 0, edge, 0.0)
    last = jnp.where(iota((8, nz), 0) == 7, -edge, 0.0)
    for p in range(planes):
        low = get_row(y_in, 0, planes, p, nz)
        low_edge = get_row(y_in, nz // 128 * planes, planes, p, nz)
        high = get_row(y_in, half, planes, p, nz)
        high_edge = get_row(y_in, half + nz // 128 * planes, planes, p, nz)
        part = slice(p * ny, (p + 1) * ny)
        dy[part, :] = own_y[part, :] + (from_prev_y * low + from_next_y * high)
        dy[p * ny:p * ny + 8, :] += first * low_edge
        dy[(p + 1) * ny - 8:(p + 1) * ny, :] += last * high_edge
        store(dy, dy_hbm, p, y_sem)
    for copy in copies:
        copy.wait()


def per_device(velocity):
    planes = velocity.shape[0] * velocity.shape[1]
    ny, nz = velocity.shape[2:]
    flat = (planes * ny, nz)
    half = (2 * planes * (nz // 128) + 7) // 8 * 8
    block = pltpu.VMEM(flat, jnp.float32)
    y_message = pltpu.VMEM((2 * half, 128), jnp.float32)
    z_message = pltpu.VMEM((16, planes * ny), jnp.float32)
    in_vmem = pl.BlockSpec(memory_space=pltpu.VMEM)
    in_hbm = pl.BlockSpec(memory_space=pltpu.HBM)
    parts = pl.pallas_call(
        functools.partial(exchange, planes),
        out_shape=(block, block, y_message, pltpu.VMEM((2 * ny, nz), jnp.float32)),
        in_specs=[in_hbm],
        out_specs=(in_vmem,) * 4,
        scratch_shapes=[
            block, y_message, z_message, z_message,
            pltpu.SemaphoreType.DMA((planes,)),
            pltpu.SemaphoreType.DMA((4,)),
            pltpu.SemaphoreType.DMA((4,)),
        ],
        compiler_params=pltpu.CompilerParams(
            collective_id=0, has_side_effects=True, vmem_limit_bytes=16 * 2**20
        ),
    )(pltpu.with_memory_space_constraint(velocity.reshape(flat), pltpu.HBM))
    stored = pltpu.HBM(flat, jnp.float32)
    deriv_y, deriv_z = pl.pallas_call(
        functools.partial(finish, planes),
        out_shape=(stored, stored),
        in_specs=[in_vmem] * 4,
        out_specs=(in_hbm, in_hbm),
        scratch_shapes=[
            block,
            pltpu.SemaphoreType.DMA((planes,)),
            pltpu.SemaphoreType.DMA((planes,)),
        ],
        compiler_params=pltpu.CompilerParams(vmem_limit_bytes=16 * 2**20),
    )(*(pltpu.with_memory_space_constraint(part, pltpu.VMEM) for part in parts))
    return deriv_y.reshape(velocity.shape), deriv_z.reshape(velocity.shape)


def solution(mesh):
    spec = P(None, None, "gy", "gz")
    return jax.shard_map(
        per_device, mesh=mesh, in_specs=(spec,), out_specs=(spec, spec), check_vma=False
    )
```

```python
import functools
import math

import jax
import jax.numpy as jnp
from jax import lax
from jax.experimental import pallas as pl
from jax.experimental.pallas import tpu as pltpu
from jax.sharding import PartitionSpec as P

MESH = pl.DeviceIdType.MESH
ratio = 1.5 - math.sqrt(5.0) / 2.0
near = 7.0 / 9.0
far = 1.0 / 36.0
green = 1.0 / (1.0 - 2.0 / 3.0 * ratio)
tail = green * (near * (1.0 / ratio - ratio) + far * (ratio**2 - 1.0 / ratio**2))
edge = far * green * (ratio - 1.0 / ratio)
log_ratio = math.log(ratio)


def powers(count):
    size = jnp.exp(count.astype(jnp.float32) * log_ratio)
    return jnp.where((count & 1) == 0, size, -size)


def weights(d):
    size = jnp.abs(d)
    value = tail * powers(size) + jnp.where(size == 1, edge, 0.0)
    return jnp.where(d > 0, value, jnp.where(d < 0, -value, 0.0))


def iota(shape, dim):
    return lax.broadcasted_iota(jnp.int32, shape, dim)


def split(x):
    high = x.astype(jnp.bfloat16)
    return high, (x - high.astype(jnp.float32)).astype(jnp.bfloat16)


def dot(a, b, dims=((1,), (0,))):
    return lax.dot_general(a, b, (dims, ((), ())), preferred_element_type=jnp.float32)


def put_row(ref, start, planes, p, row):
    for c in range(row.shape[1] // 128):
        place = start + c * planes + p
        ref[place:place + 1, :] = row[:, c * 128:(c + 1) * 128]


def get_row(ref, start, planes, p, nz):
    places = [start + c * planes + p for c in range(nz // 128)]
    return jnp.concatenate([ref[place:place + 1, :] for place in places], axis=1)


def exchange(planes, v_hbm, dy, dz, y_in, y_weight, v, y_out, z_out, z_in, load_sem, send_sem, recv_sem, ready_sem):
    rows, nz = v.shape
    ny = rows // planes
    half = y_out.shape[0] // 2
    gy, gz = lax.axis_size("gy"), lax.axis_size("gz")
    iy, iz = lax.axis_index("gy"), lax.axis_index("gz")
    y_next = (lax.rem(iy + 1, gy), iz)
    y_prev = (lax.rem(iy + gy - 1, gy), iz)
    z_next = (iy, lax.rem(iz + 1, gz))
    z_prev = (iy, lax.rem(iz + gz - 1, gz))

    odd = lax.rem(iy, 2) == 1
    even = lax.rem(iy, 2) == 0
    barrier = pltpu.get_barrier_semaphore()

    def greet(*others):
        for other in others:
            pl.semaphore_signal(barrier, inc=1, device_id=other, device_id_type=MESH)

    @pl.when(even)
    def _():
        greet(y_prev, y_next)

    greet(z_prev, z_next)
    loads = []
    for p in range(planes):
        part = pl.ds(p * ny, ny)
        loads.append(pltpu.make_async_copy(v_hbm.at[part], v.at[part], load_sem.at[p]))
        loads[-1].start()

    def message_to(index, source, target, start, count, other):
        return pltpu.make_async_remote_copy(
            src_ref=source.at[pl.ds(start, count)],
            dst_ref=target.at[pl.ds(start, count)],
            send_sem=send_sem.at[index],
            recv_sem=recv_sem.at[index],
            device_id=other,
            device_id_type=MESH,
        )

    place = iota((ny, 128), 0)
    to_next_y = jnp.concatenate([powers(ny - 1 - place)] * (nz // 128), axis=1)
    to_prev_y = jnp.concatenate([powers(place)] * (nz // 128), axis=1)
    which, k = iota((16, nz), 0), iota((16, nz), 1)
    message = jnp.where(which == 0, powers(nz - 1 - k), 0.0)
    message = jnp.where((which == 1) & (k == nz - 1), 1.0, message)
    message = jnp.where(which == 8, powers(k), message)
    message = jnp.where((which == 9) & (k == 0), 1.0, message)
    message_hi, message_lo = split(message)
    message_both = jnp.concatenate([message_hi, message_lo], axis=0)
    y_hi, y_lo = split(weights(iota((ny, ny), 0) - iota((ny, ny), 1)))
    z_hi, z_lo = split(weights(iota((nz, nz), 1) - iota((nz, nz), 0)))

    spread = jnp.where(which == 0, tail * powers(k + 1), 0.0)
    spread = jnp.where((which == 1) & (k == 0), edge, spread)
    spread = jnp.where(which == 8, -tail * powers(nz - k), spread)
    spread = jnp.where((which == 9) & (k == nz - 1), -edge, spread)
    spread_hi, spread_lo = split(spread)
    if half > 2 * planes * (nz // 128):
        y_out[...] = jnp.zeros_like(y_out)
    y_weight[:ny, :] = -tail * ratio * to_prev_y
    y_weight[ny:, :] = tail * ratio * to_next_y

    for p in range(planes):
        loads[p].wait()
        plane = v[p * ny:(p + 1) * ny, :]
        put_row(y_out, 0, planes, p, jnp.sum(plane * to_next_y, axis=0, keepdims=True))
        put_row(y_out, nz // 128 * planes, planes, p, plane[ny - 1:ny, :])
        put_row(y_out, half, planes, p, jnp.sum(plane * to_prev_y, axis=0, keepdims=True))
        put_row(y_out, half + nz // 128 * planes, planes, p, plane[0:1, :])
    v_hi, v_lo = split(v[...])
    nt = ((1,), (1,))
    both = dot(message_both, v_hi, nt)
    z_out[...] = both[:16] + (both[16:] + dot(message_hi, v_lo, nt))
    copies = [
        message_to(0, y_out, y_in, 0, half, y_next),
        message_to(1, y_out, y_in, half, half, y_prev),
        message_to(2, z_out, z_in, 0, 8, z_next),
        message_to(3, z_out, z_in, 8, 8, z_prev),
    ]

    @pl.when(odd)
    def _():
        pl.semaphore_wait(barrier, 4)
        pl.semaphore_signal(ready_sem.at[0], inc=1, device_id=y_prev, device_id_type=MESH)
        pl.semaphore_signal(ready_sem.at[1], inc=1, device_id=y_next, device_id_type=MESH)
        copies[0].start()
        copies[1].start()

    @pl.when(even)
    def _():
        pl.semaphore_wait(barrier, 2)

    copies[2].start()
    copies[3].start()

    for p in range(planes):
        plane_hi = v_hi[p * ny:(p + 1) * ny, :]
        plane_lo = v_lo[p * ny:(p + 1) * ny, :]
        dy[p * ny:(p + 1) * ny, :] = dot(y_hi, plane_hi) + (dot(y_lo, plane_hi) + dot(y_hi, plane_lo))
    dz[...] = dot(v_hi, z_hi) + (dot(v_lo, z_hi) + dot(v_hi, z_lo))

    copies[2].wait_recv()
    copies[3].wait_recv()
    in_hi, in_lo = split(z_in[...])
    dz[...] += dot(
        jnp.concatenate([in_hi, in_lo, in_hi], axis=0),
        jnp.concatenate([spread_hi, spread_hi, spread_lo], axis=0),
        ((0,), (0,)),
    )

    @pl.when(even)
    def _():
        pl.semaphore_wait(ready_sem.at[0], 1)
        copies[0].start()
        pl.semaphore_wait(ready_sem.at[1], 1)
        copies[1].start()

    copies[0].wait_recv()
    copies[1].wait_recv()
    for copy in copies:
        copy.wait_send()


def finish(planes, own_y, dz, y_in, y_weight, dy_hbm, dz_hbm, dy, y_sem, z_sem):
    rows, nz = own_y.shape
    ny = rows // planes
    half = y_in.shape[0] // 2
    copies = []

    def store(source, target, p, sem):
        part = pl.ds(p * ny, ny)
        copies.append(pltpu.make_async_copy(source.at[part], target.at[part], sem.at[p]))
        copies[-1].start()

    for p in range(planes):
        store(dz, dz_hbm, p, z_sem)
    from_prev_y, from_next_y = y_weight[:ny, :], y_weight[ny:, :]
    first = jnp.where(iota((8, nz), 0) == 0, edge, 0.0)
    last = jnp.where(iota((8, nz), 0) == 7, -edge, 0.0)
    for p in range(planes):
        low = get_row(y_in, 0, planes, p, nz)
        low_edge = get_row(y_in, nz // 128 * planes, planes, p, nz)
        high = get_row(y_in, half, planes, p, nz)
        high_edge = get_row(y_in, half + nz // 128 * planes, planes, p, nz)
        part = slice(p * ny, (p + 1) * ny)
        dy[part, :] = own_y[part, :] + (from_prev_y * low + from_next_y * high)
        dy[p * ny:p * ny + 8, :] += first * low_edge
        dy[(p + 1) * ny - 8:(p + 1) * ny, :] += last * high_edge
        store(dy, dy_hbm, p, y_sem)
    for copy in copies:
        copy.wait()


def per_device(velocity):
    planes = velocity.shape[0] * velocity.shape[1]
    ny, nz = velocity.shape[2:]
    flat = (planes * ny, nz)
    half = (2 * planes * (nz // 128) + 7) // 8 * 8
    block = pltpu.VMEM(flat, jnp.float32)
    y_message = pltpu.VMEM((2 * half, 128), jnp.float32)
    z_message = pltpu.VMEM((16, planes * ny), jnp.float32)
    in_vmem = pl.BlockSpec(memory_space=pltpu.VMEM)
    in_hbm = pl.BlockSpec(memory_space=pltpu.HBM)
    parts = pl.pallas_call(
        functools.partial(exchange, planes),
        out_shape=(block, block, y_message, pltpu.VMEM((2 * ny, nz), jnp.float32)),
        in_specs=[in_hbm],
        out_specs=(in_vmem,) * 4,
        scratch_shapes=[
            block, y_message, z_message, z_message,
            pltpu.SemaphoreType.DMA((planes,)),
            pltpu.SemaphoreType.DMA((4,)),
            pltpu.SemaphoreType.DMA((4,)),
            pltpu.SemaphoreType.REGULAR((2,)),
        ],
        compiler_params=pltpu.CompilerParams(
            collective_id=0, has_side_effects=True, vmem_limit_bytes=16 * 2**20
        ),
    )(pltpu.with_memory_space_constraint(velocity.reshape(flat), pltpu.HBM))
    stored = pltpu.HBM(flat, jnp.float32)
    deriv_y, deriv_z = pl.pallas_call(
        functools.partial(finish, planes),
        out_shape=(stored, stored),
        in_specs=[in_vmem] * 4,
        out_specs=(in_hbm, in_hbm),
        scratch_shapes=[
            block,
            pltpu.SemaphoreType.DMA((planes,)),
            pltpu.SemaphoreType.DMA((planes,)),
        ],
        compiler_params=pltpu.CompilerParams(vmem_limit_bytes=16 * 2**20),
    )(*(pltpu.with_memory_space_constraint(part, pltpu.VMEM) for part in parts))
    return deriv_y.reshape(velocity.shape), deriv_z.reshape(velocity.shape)


def solution(mesh):
    spec = P(None, None, "gy", "gz")
    return jax.shard_map(
        per_device, mesh=mesh, in_specs=(spec,), out_specs=(spec, spec), check_vma=False
    )
```

```python
import functools
import math

import jax
import jax.numpy as jnp
from jax import lax
from jax.experimental import pallas as pl
from jax.experimental.pallas import tpu as pltpu
from jax.sharding import PartitionSpec as P

MESH = pl.DeviceIdType.MESH
ratio = 1.5 - math.sqrt(5.0) / 2.0
near = 7.0 / 9.0
far = 1.0 / 36.0
green = 1.0 / (1.0 - 2.0 / 3.0 * ratio)
tail = green * (near * (1.0 / ratio - ratio) + far * (ratio**2 - 1.0 / ratio**2))
edge = far * green * (ratio - 1.0 / ratio)
log_ratio = math.log(ratio)


def powers(count):
    size = jnp.exp(count.astype(jnp.float32) * log_ratio)
    return jnp.where((count & 1) == 0, size, -size)


def weights(d):
    size = jnp.abs(d)
    value = tail * powers(size) + jnp.where(size == 1, edge, 0.0)
    return jnp.where(d > 0, value, jnp.where(d < 0, -value, 0.0))


def iota(shape, dim):
    return lax.broadcasted_iota(jnp.int32, shape, dim)


def split(x):
    high = x.astype(jnp.bfloat16)
    return high, (x - high.astype(jnp.float32)).astype(jnp.bfloat16)


def dot(a, b, dims=((1,), (0,))):
    return lax.dot_general(a, b, (dims, ((), ())), preferred_element_type=jnp.float32)


def put_row(ref, start, planes, p, row):
    for c in range(row.shape[1] // 128):
        place = start + c * planes + p
        ref[place:place + 1, :] = row[:, c * 128:(c + 1) * 128]


def get_row(ref, start, planes, p, nz):
    places = [start + c * planes + p for c in range(nz // 128)]
    return jnp.concatenate([ref[place:place + 1, :] for place in places], axis=1)


def exchange(planes, v_hbm, dy, dz, y_in, y_weight, v, y_out, z_out, z_in, load_sem, send_sem, recv_sem, ready_sem):
    rows, nz = v.shape
    ny = rows // planes
    half = y_out.shape[0] // 2
    gy, gz = lax.axis_size("gy"), lax.axis_size("gz")
    iy, iz = lax.axis_index("gy"), lax.axis_index("gz")
    y_next = (lax.rem(iy + 1, gy), iz)
    y_prev = (lax.rem(iy + gy - 1, gy), iz)
    z_next = (iy, lax.rem(iz + 1, gz))
    z_prev = (iy, lax.rem(iz + gz - 1, gz))

    odd_row = lax.rem(iy, 2) == 1
    even_row = lax.rem(iy, 2) == 0
    quick = odd_row & (lax.rem(iz, 2) == 0)
    full = odd_row & (lax.rem(iz, 2) == 1)
    barrier = pltpu.get_barrier_semaphore()

    def signal(sem, other):
        pl.semaphore_signal(sem, inc=1, device_id=other, device_id_type=MESH)

    @pl.when(even_row)
    def _():
        signal(barrier, y_prev)
        signal(barrier, y_next)

    @pl.when(even_row | quick)
    def _():
        signal(barrier, z_prev)
        signal(barrier, z_next)

    loads = []
    for p in range(planes):
        part = pl.ds(p * ny, ny)
        loads.append(pltpu.make_async_copy(v_hbm.at[part], v.at[part], load_sem.at[p]))
        loads[-1].start()

    def message_to(index, source, target, start, count, other):
        return pltpu.make_async_remote_copy(
            src_ref=source.at[pl.ds(start, count)],
            dst_ref=target.at[pl.ds(start, count)],
            send_sem=send_sem.at[index],
            recv_sem=recv_sem.at[index],
            device_id=other,
            device_id_type=MESH,
        )

    place = iota((ny, 128), 0)
    to_next_y = jnp.concatenate([powers(ny - 1 - place)] * (nz // 128), axis=1)
    to_prev_y = jnp.concatenate([powers(place)] * (nz // 128), axis=1)
    which, k = iota((16, nz), 0), iota((16, nz), 1)
    message = jnp.where(which == 0, powers(nz - 1 - k), 0.0)
    message = jnp.where((which == 1) & (k == nz - 1), 1.0, message)
    message = jnp.where(which == 8, powers(k), message)
    message = jnp.where((which == 9) & (k == 0), 1.0, message)
    message_hi, message_lo = split(message)
    message_both = jnp.concatenate([message_hi, message_lo], axis=0)
    y_hi, y_lo = split(weights(iota((ny, ny), 0) - iota((ny, ny), 1)))
    z_hi, z_lo = split(weights(iota((nz, nz), 1) - iota((nz, nz), 0)))

    spread = jnp.where(which == 0, tail * powers(k + 1), 0.0)
    spread = jnp.where((which == 1) & (k == 0), edge, spread)
    spread = jnp.where(which == 8, -tail * powers(nz - k), spread)
    spread = jnp.where((which == 9) & (k == nz - 1), -edge, spread)
    spread_hi, spread_lo = split(spread)
    if half > 2 * planes * (nz // 128):
        y_out[...] = jnp.zeros_like(y_out)
    y_weight[:ny, :] = -tail * ratio * to_prev_y
    y_weight[ny:, :] = tail * ratio * to_next_y

    for p in range(planes):
        loads[p].wait()
        plane = v[p * ny:(p + 1) * ny, :]
        put_row(y_out, 0, planes, p, jnp.sum(plane * to_next_y, axis=0, keepdims=True))
        put_row(y_out, nz // 128 * planes, planes, p, plane[ny - 1:ny, :])
        put_row(y_out, half, planes, p, jnp.sum(plane * to_prev_y, axis=0, keepdims=True))
        put_row(y_out, half + nz // 128 * planes, planes, p, plane[0:1, :])
    v_hi, v_lo = split(v[...])
    nt = ((1,), (1,))
    both = dot(message_both, v_hi, nt)
    z_out[...] = both[:16] + (both[16:] + dot(message_hi, v_lo, nt))
    copies = [
        message_to(0, y_out, y_in, 0, half, y_next),
        message_to(1, y_out, y_in, half, half, y_prev),
        message_to(2, z_out, z_in, 0, 8, z_next),
        message_to(3, z_out, z_in, 8, 8, z_prev),
    ]

    @pl.when(full)
    def _():
        pl.semaphore_wait(barrier, 4)

    @pl.when(even_row | quick)
    def _():
        pl.semaphore_wait(barrier, 2)

    @pl.when(odd_row)
    def _():
        signal(ready_sem.at[0], y_prev)
        signal(ready_sem.at[1], y_next)
        copies[0].start()
        copies[1].start()

    @pl.when(full)
    def _():
        signal(ready_sem.at[2], z_prev)
        signal(ready_sem.at[3], z_next)

    @pl.when(even_row | full)
    def _():
        copies[2].start()
        copies[3].start()

    for p in range(planes):
        plane_hi = v_hi[p * ny:(p + 1) * ny, :]
        plane_lo = v_lo[p * ny:(p + 1) * ny, :]
        dy[p * ny:(p + 1) * ny, :] = dot(y_hi, plane_hi) + (dot(y_lo, plane_hi) + dot(y_hi, plane_lo))
    dz[...] = dot(v_hi, z_hi) + (dot(v_lo, z_hi) + dot(v_hi, z_lo))

    @pl.when(quick)
    def _():
        pl.semaphore_wait(ready_sem.at[2], 1)
        copies[2].start()
        pl.semaphore_wait(ready_sem.at[3], 1)
        copies[3].start()

    copies[2].wait_recv()
    copies[3].wait_recv()
    in_hi, in_lo = split(z_in[...])
    dz[...] += dot(
        jnp.concatenate([in_hi, in_lo, in_hi], axis=0),
        jnp.concatenate([spread_hi, spread_hi, spread_lo], axis=0),
        ((0,), (0,)),
    )

    @pl.when(even_row)
    def _():
        pl.semaphore_wait(ready_sem.at[0], 1)
        copies[0].start()
        pl.semaphore_wait(ready_sem.at[1], 1)
        copies[1].start()

    copies[0].wait_recv()
    copies[1].wait_recv()
    for copy in copies:
        copy.wait_send()


def finish(planes, own_y, dz, y_in, y_weight, dy_hbm, dz_hbm, dy, y_sem, z_sem):
    rows, nz = own_y.shape
    ny = rows // planes
    half = y_in.shape[0] // 2
    copies = []

    def store(source, target, p, sem):
        part = pl.ds(p * ny, ny)
        copies.append(pltpu.make_async_copy(source.at[part], target.at[part], sem.at[p]))
        copies[-1].start()

    for p in range(planes):
        store(dz, dz_hbm, p, z_sem)
    from_prev_y, from_next_y = y_weight[:ny, :], y_weight[ny:, :]
    first = jnp.where(iota((8, nz), 0) == 0, edge, 0.0)
    last = jnp.where(iota((8, nz), 0) == 7, -edge, 0.0)
    for p in range(planes):
        low = get_row(y_in, 0, planes, p, nz)
        low_edge = get_row(y_in, nz // 128 * planes, planes, p, nz)
        high = get_row(y_in, half, planes, p, nz)
        high_edge = get_row(y_in, half + nz // 128 * planes, planes, p, nz)
        part = slice(p * ny, (p + 1) * ny)
        dy[part, :] = own_y[part, :] + (from_prev_y * low + from_next_y * high)
        dy[p * ny:p * ny + 8, :] += first * low_edge
        dy[(p + 1) * ny - 8:(p + 1) * ny, :] += last * high_edge
        store(dy, dy_hbm, p, y_sem)
    for copy in copies:
        copy.wait()


def per_device(velocity):
    planes = velocity.shape[0] * velocity.shape[1]
    ny, nz = velocity.shape[2:]
    flat = (planes * ny, nz)
    half = (2 * planes * (nz // 128) + 7) // 8 * 8
    block = pltpu.VMEM(flat, jnp.float32)
    y_message = pltpu.VMEM((2 * half, 128), jnp.float32)
    z_message = pltpu.VMEM((16, planes * ny), jnp.float32)
    in_vmem = pl.BlockSpec(memory_space=pltpu.VMEM)
    in_hbm = pl.BlockSpec(memory_space=pltpu.HBM)
    parts = pl.pallas_call(
        functools.partial(exchange, planes),
        out_shape=(block, block, y_message, pltpu.VMEM((2 * ny, nz), jnp.float32)),
        in_specs=[in_hbm],
        out_specs=(in_vmem,) * 4,
        scratch_shapes=[
            block, y_message, z_message, z_message,
            pltpu.SemaphoreType.DMA((planes,)),
            pltpu.SemaphoreType.DMA((4,)),
            pltpu.SemaphoreType.DMA((4,)),
            pltpu.SemaphoreType.REGULAR((4,)),
        ],
        compiler_params=pltpu.CompilerParams(
            collective_id=0, has_side_effects=True, vmem_limit_bytes=16 * 2**20
        ),
    )(pltpu.with_memory_space_constraint(velocity.reshape(flat), pltpu.HBM))
    stored = pltpu.HBM(flat, jnp.float32)
    deriv_y, deriv_z = pl.pallas_call(
        functools.partial(finish, planes),
        out_shape=(stored, stored),
        in_specs=[in_vmem] * 4,
        out_specs=(in_hbm, in_hbm),
        scratch_shapes=[
            block,
            pltpu.SemaphoreType.DMA((planes,)),
            pltpu.SemaphoreType.DMA((planes,)),
        ],
        compiler_params=pltpu.CompilerParams(vmem_limit_bytes=16 * 2**20),
    )(*(pltpu.with_memory_space_constraint(part, pltpu.VMEM) for part in parts))
    return deriv_y.reshape(velocity.shape), deriv_z.reshape(velocity.shape)


def solution(mesh):
    spec = P(None, None, "gy", "gz")
    return jax.shard_map(
        per_device, mesh=mesh, in_specs=(spec,), out_specs=(spec, spec), check_vma=False
    )
```

```python
import functools
import math

import jax
import jax.numpy as jnp
from jax import lax
from jax.experimental import pallas as pl
from jax.experimental.pallas import tpu as pltpu
from jax.sharding import PartitionSpec as P

MESH = pl.DeviceIdType.MESH
ratio = 1.5 - math.sqrt(5.0) / 2.0
near = 7.0 / 9.0
far = 1.0 / 36.0
green = 1.0 / (1.0 - 2.0 / 3.0 * ratio)
tail = green * (near * (1.0 / ratio - ratio) + far * (ratio**2 - 1.0 / ratio**2))
edge = far * green * (ratio - 1.0 / ratio)
log_ratio = math.log(ratio)


def powers(count):
    size = jnp.exp(count.astype(jnp.float32) * log_ratio)
    return jnp.where((count & 1) == 0, size, -size)


def weights(d):
    size = jnp.abs(d)
    value = tail * powers(size) + jnp.where(size == 1, edge, 0.0)
    return jnp.where(d > 0, value, jnp.where(d < 0, -value, 0.0))


def iota(shape, dim):
    return lax.broadcasted_iota(jnp.int32, shape, dim)


def split(x):
    high = x.astype(jnp.bfloat16)
    return high, (x - high.astype(jnp.float32)).astype(jnp.bfloat16)


def dot(a, b, dims=((1,), (0,))):
    return lax.dot_general(a, b, (dims, ((), ())), preferred_element_type=jnp.float32)


def put_row(ref, start, planes, p, row):
    for c in range(row.shape[1] // 128):
        place = start + c * planes + p
        ref[place:place + 1, :] = row[:, c * 128:(c + 1) * 128]


def get_row(ref, start, planes, p, nz):
    places = [start + c * planes + p for c in range(nz // 128)]
    return jnp.concatenate([ref[place:place + 1, :] for place in places], axis=1)


def exchange(planes, v_hbm, dy, dz, y_in, y_weight, v, y_out, z_out, z_in, load_sem, send_sem, recv_sem, ready_sem):
    rows, nz = v.shape
    ny = rows // planes
    half = y_out.shape[0] // 2
    gy, gz = lax.axis_size("gy"), lax.axis_size("gz")
    iy, iz = lax.axis_index("gy"), lax.axis_index("gz")
    y_next = (lax.rem(iy + 1, gy), iz)
    y_prev = (lax.rem(iy + gy - 1, gy), iz)
    z_next = (iy, lax.rem(iz + 1, gz))
    z_prev = (iy, lax.rem(iz + gz - 1, gz))

    odd_row = lax.rem(iy, 2) == 1
    even_row = lax.rem(iy, 2) == 0
    quick = odd_row & (lax.rem(iz, 2) == 0)
    full = odd_row & (lax.rem(iz, 2) == 1)
    barrier = pltpu.get_barrier_semaphore()

    def signal(sem, other):
        pl.semaphore_signal(sem, inc=1, device_id=other, device_id_type=MESH)

    @pl.when(even_row)
    def _():
        signal(barrier, y_prev)
        signal(barrier, y_next)

    @pl.when(even_row | quick)
    def _():
        signal(barrier, z_prev)
        signal(barrier, z_next)

    loads = []
    for p in range(planes):
        part = pl.ds(p * ny, ny)
        loads.append(pltpu.make_async_copy(v_hbm.at[part], v.at[part], load_sem.at[p]))
        loads[-1].start()

    def message_to(index, source, target, start, count, other):
        return pltpu.make_async_remote_copy(
            src_ref=source.at[pl.ds(start, count)],
            dst_ref=target.at[pl.ds(start, count)],
            send_sem=send_sem.at[index],
            recv_sem=recv_sem.at[index],
            device_id=other,
            device_id_type=MESH,
        )

    place = iota((ny, 128), 0)
    to_next_y = jnp.concatenate([powers(ny - 1 - place)] * (nz // 128), axis=1)
    to_prev_y = jnp.concatenate([powers(place)] * (nz // 128), axis=1)
    which, k = iota((16, nz), 0), iota((16, nz), 1)
    message = jnp.where(which == 0, powers(nz - 1 - k), 0.0)
    message = jnp.where((which == 1) & (k == nz - 1), 1.0, message)
    message = jnp.where(which == 8, powers(k), message)
    message = jnp.where((which == 9) & (k == 0), 1.0, message)
    message_hi, message_lo = split(message)
    message_both = jnp.concatenate([message_hi, message_lo], axis=0)
    if half > 2 * planes * (nz // 128):
        y_out[...] = jnp.zeros_like(y_out)
    for p in range(planes):
        loads[p].wait()
        plane = v[p * ny:(p + 1) * ny, :]
        put_row(y_out, 0, planes, p, jnp.sum(plane * to_next_y, axis=0, keepdims=True))
        put_row(y_out, nz // 128 * planes, planes, p, plane[ny - 1:ny, :])
        put_row(y_out, half, planes, p, jnp.sum(plane * to_prev_y, axis=0, keepdims=True))
        put_row(y_out, half + nz // 128 * planes, planes, p, plane[0:1, :])
    copies = [
        message_to(0, y_out, y_in, 0, half, y_next),
        message_to(1, y_out, y_in, half, half, y_prev),
        message_to(2, z_out, z_in, 0, 8, z_next),
        message_to(3, z_out, z_in, 8, 8, z_prev),
    ]

    def send_y():
        signal(ready_sem.at[0], y_prev)
        signal(ready_sem.at[1], y_next)
        copies[0].start()
        copies[1].start()

    @pl.when(quick)
    def _():
        pl.semaphore_wait(barrier, 2)
        send_y()

    v_hi, v_lo = split(v[...])
    nt = ((1,), (1,))
    both = dot(message_both, v_hi, nt)
    z_out[...] = both[:16] + (both[16:] + dot(message_hi, v_lo, nt))

    @pl.when(even_row)
    def _():
        pl.semaphore_wait(barrier, 2)

    @pl.when(full)
    def _():
        pl.semaphore_wait(barrier, 4)
        send_y()
        signal(ready_sem.at[2], z_prev)
        signal(ready_sem.at[3], z_next)

    @pl.when(even_row | full)
    def _():
        copies[2].start()
        copies[3].start()

    y_hi, y_lo = split(weights(iota((ny, ny), 0) - iota((ny, ny), 1)))
    z_hi, z_lo = split(weights(iota((nz, nz), 1) - iota((nz, nz), 0)))

    spread = jnp.where(which == 0, tail * powers(k + 1), 0.0)
    spread = jnp.where((which == 1) & (k == 0), edge, spread)
    spread = jnp.where(which == 8, -tail * powers(nz - k), spread)
    spread = jnp.where((which == 9) & (k == nz - 1), -edge, spread)
    spread_hi, spread_lo = split(spread)
    y_weight[:ny, :] = -tail * ratio * to_prev_y
    y_weight[ny:, :] = tail * ratio * to_next_y

    for p in range(planes):
        plane_hi = v_hi[p * ny:(p + 1) * ny, :]
        plane_lo = v_lo[p * ny:(p + 1) * ny, :]
        dy[p * ny:(p + 1) * ny, :] = dot(y_hi, plane_hi) + (dot(y_lo, plane_hi) + dot(y_hi, plane_lo))
    dz[...] = dot(v_hi, z_hi) + (dot(v_lo, z_hi) + dot(v_hi, z_lo))

    @pl.when(quick)
    def _():
        pl.semaphore_wait(ready_sem.at[2], 1)
        copies[2].start()
        pl.semaphore_wait(ready_sem.at[3], 1)
        copies[3].start()

    copies[2].wait_recv()
    copies[3].wait_recv()
    in_hi, in_lo = split(z_in[...])
    dz[...] += dot(
        jnp.concatenate([in_hi, in_lo, in_hi], axis=0),
        jnp.concatenate([spread_hi, spread_hi, spread_lo], axis=0),
        ((0,), (0,)),
    )

    @pl.when(even_row)
    def _():
        pl.semaphore_wait(ready_sem.at[0], 1)
        copies[0].start()
        pl.semaphore_wait(ready_sem.at[1], 1)
        copies[1].start()

    copies[0].wait_recv()
    copies[1].wait_recv()
    for copy in copies:
        copy.wait_send()


def finish(planes, own_y, dz, y_in, y_weight, dy_hbm, dz_hbm, dy, y_sem, z_sem):
    rows, nz = own_y.shape
    ny = rows // planes
    half = y_in.shape[0] // 2
    copies = []

    def store(source, target, p, sem):
        part = pl.ds(p * ny, ny)
        copies.append(pltpu.make_async_copy(source.at[part], target.at[part], sem.at[p]))
        copies[-1].start()

    for p in range(planes):
        store(dz, dz_hbm, p, z_sem)
    from_prev_y, from_next_y = y_weight[:ny, :], y_weight[ny:, :]
    first = jnp.where(iota((8, nz), 0) == 0, edge, 0.0)
    last = jnp.where(iota((8, nz), 0) == 7, -edge, 0.0)
    for p in range(planes):
        low = get_row(y_in, 0, planes, p, nz)
        low_edge = get_row(y_in, nz // 128 * planes, planes, p, nz)
        high = get_row(y_in, half, planes, p, nz)
        high_edge = get_row(y_in, half + nz // 128 * planes, planes, p, nz)
        part = slice(p * ny, (p + 1) * ny)
        dy[part, :] = own_y[part, :] + (from_prev_y * low + from_next_y * high)
        dy[p * ny:p * ny + 8, :] += first * low_edge
        dy[(p + 1) * ny - 8:(p + 1) * ny, :] += last * high_edge
        store(dy, dy_hbm, p, y_sem)
    for copy in copies:
        copy.wait()


def per_device(velocity):
    planes = velocity.shape[0] * velocity.shape[1]
    ny, nz = velocity.shape[2:]
    flat = (planes * ny, nz)
    half = (2 * planes * (nz // 128) + 7) // 8 * 8
    block = pltpu.VMEM(flat, jnp.float32)
    y_message = pltpu.VMEM((2 * half, 128), jnp.float32)
    z_message = pltpu.VMEM((16, planes * ny), jnp.float32)
    in_vmem = pl.BlockSpec(memory_space=pltpu.VMEM)
    in_hbm = pl.BlockSpec(memory_space=pltpu.HBM)
    parts = pl.pallas_call(
        functools.partial(exchange, planes),
        out_shape=(block, block, y_message, pltpu.VMEM((2 * ny, nz), jnp.float32)),
        in_specs=[in_hbm],
        out_specs=(in_vmem,) * 4,
        scratch_shapes=[
            block, y_message, z_message, z_message,
            pltpu.SemaphoreType.DMA((planes,)),
            pltpu.SemaphoreType.DMA((4,)),
            pltpu.SemaphoreType.DMA((4,)),
            pltpu.SemaphoreType.REGULAR((4,)),
        ],
        compiler_params=pltpu.CompilerParams(
            collective_id=0, has_side_effects=True, vmem_limit_bytes=16 * 2**20
        ),
    )(pltpu.with_memory_space_constraint(velocity.reshape(flat), pltpu.HBM))
    stored = pltpu.HBM(flat, jnp.float32)
    deriv_y, deriv_z = pl.pallas_call(
        functools.partial(finish, planes),
        out_shape=(stored, stored),
        in_specs=[in_vmem] * 4,
        out_specs=(in_hbm, in_hbm),
        scratch_shapes=[
            block,
            pltpu.SemaphoreType.DMA((planes,)),
            pltpu.SemaphoreType.DMA((planes,)),
        ],
        compiler_params=pltpu.CompilerParams(vmem_limit_bytes=16 * 2**20),
    )(*(pltpu.with_memory_space_constraint(part, pltpu.VMEM) for part in parts))
    return deriv_y.reshape(velocity.shape), deriv_z.reshape(velocity.shape)


def solution(mesh):
    spec = P(None, None, "gy", "gz")
    return jax.shard_map(
        per_device, mesh=mesh, in_specs=(spec,), out_specs=(spec, spec), check_vma=False
    )
```

```python
import functools
import math

import jax
import jax.numpy as jnp
from jax import lax
from jax.experimental import pallas as pl
from jax.experimental.pallas import tpu as pltpu
from jax.sharding import PartitionSpec as P

MESH = pl.DeviceIdType.MESH
ratio = 1.5 - math.sqrt(5.0) / 2.0
near = 7.0 / 9.0
far = 1.0 / 36.0
green = 1.0 / (1.0 - 2.0 / 3.0 * ratio)
tail = green * (near * (1.0 / ratio - ratio) + far * (ratio**2 - 1.0 / ratio**2))
edge = far * green * (ratio - 1.0 / ratio)
log_ratio = math.log(ratio)


def powers(count):
    size = jnp.exp(count.astype(jnp.float32) * log_ratio)
    return jnp.where((count & 1) == 0, size, -size)


def weights(d):
    size = jnp.abs(d)
    value = tail * powers(size) + jnp.where(size == 1, edge, 0.0)
    return jnp.where(d > 0, value, jnp.where(d < 0, -value, 0.0))


def iota(shape, dim):
    return lax.broadcasted_iota(jnp.int32, shape, dim)


def split(x):
    high = x.astype(jnp.bfloat16)
    return high, (x - high.astype(jnp.float32)).astype(jnp.bfloat16)


def dot(a, b, dims=((1,), (0,))):
    return lax.dot_general(a, b, (dims, ((), ())), preferred_element_type=jnp.float32)


def put_row(ref, start, planes, p, row):
    for c in range(row.shape[1] // 128):
        place = start + c * planes + p
        ref[place:place + 1, :] = row[:, c * 128:(c + 1) * 128]


def get_row(ref, start, planes, p, nz):
    places = [start + c * planes + p for c in range(nz // 128)]
    return jnp.concatenate([ref[place:place + 1, :] for place in places], axis=1)


def exchange(planes, v_hbm, dy, dz, y_in, y_weight, v, y_out, z_out, z_in, load_sem, send_sem, recv_sem, ready_sem):
    rows, nz = v.shape
    ny = rows // planes
    half = y_out.shape[0] // 2
    gy, gz = lax.axis_size("gy"), lax.axis_size("gz")
    iy, iz = lax.axis_index("gy"), lax.axis_index("gz")
    y_next = (lax.rem(iy + 1, gy), iz)
    y_prev = (lax.rem(iy + gy - 1, gy), iz)
    z_next = (iy, lax.rem(iz + 1, gz))
    z_prev = (iy, lax.rem(iz + gz - 1, gz))

    odd_row = lax.rem(iy, 2) == 1
    even_row = lax.rem(iy, 2) == 0
    quick = odd_row & (lax.rem(iz, 2) == 0)
    full = odd_row & (lax.rem(iz, 2) == 1)
    barrier = pltpu.get_barrier_semaphore()

    def signal(sem, other):
        pl.semaphore_signal(sem, inc=1, device_id=other, device_id_type=MESH)

    @pl.when(even_row)
    def _():
        signal(barrier, y_prev)
        signal(barrier, y_next)

    @pl.when(even_row | quick)
    def _():
        signal(barrier, z_prev)
        signal(barrier, z_next)

    loads = []
    for p in range(planes):
        part = pl.ds(p * ny, ny)
        loads.append(pltpu.make_async_copy(v_hbm.at[part], v.at[part], load_sem.at[p]))
        loads[-1].start()

    def message_to(index, source, target, start, count, other):
        return pltpu.make_async_remote_copy(
            src_ref=source.at[pl.ds(start, count)],
            dst_ref=target.at[pl.ds(start, count)],
            send_sem=send_sem.at[index],
            recv_sem=recv_sem.at[index],
            device_id=other,
            device_id_type=MESH,
        )

    place = iota((ny, 128), 0)
    to_next_y = jnp.concatenate([powers(ny - 1 - place)] * (nz // 128), axis=1)
    to_prev_y = jnp.concatenate([powers(place)] * (nz // 128), axis=1)
    which, k = iota((16, nz), 0), iota((16, nz), 1)
    message = jnp.where(which == 0, powers(nz - 1 - k), 0.0)
    message = jnp.where((which == 1) & (k == nz - 1), 1.0, message)
    message = jnp.where(which == 8, powers(k), message)
    message = jnp.where((which == 9) & (k == 0), 1.0, message)
    message_hi, message_lo = split(message)
    message_both = jnp.concatenate([message_hi, message_lo], axis=0)
    if half > 2 * planes * (nz // 128):
        y_out[...] = jnp.zeros_like(y_out)
    for p in range(planes):
        loads[p].wait()
        plane = v[p * ny:(p + 1) * ny, :]
        put_row(y_out, 0, planes, p, jnp.sum(plane * to_next_y, axis=0, keepdims=True))
        put_row(y_out, nz // 128 * planes, planes, p, plane[ny - 1:ny, :])
        put_row(y_out, half, planes, p, jnp.sum(plane * to_prev_y, axis=0, keepdims=True))
        put_row(y_out, half + nz // 128 * planes, planes, p, plane[0:1, :])
    copies = [
        message_to(0, y_out, y_in, 0, half, y_next),
        message_to(1, y_out, y_in, half, half, y_prev),
        message_to(2, z_out, z_in, 0, 8, z_next),
        message_to(3, z_out, z_in, 8, 8, z_prev),
    ]

    def send_y():
        signal(ready_sem.at[1], y_next)
        copies[0].start()
        signal(ready_sem.at[0], y_prev)
        copies[1].start()

    @pl.when(quick)
    def _():
        pl.semaphore_wait(barrier, 2)
        send_y()

    v_hi, v_lo = split(v[...])
    nt = ((1,), (1,))
    both = dot(message_both, v_hi, nt)
    z_out[...] = both[:16] + (both[16:] + dot(message_hi, v_lo, nt))

    @pl.when(even_row)
    def _():
        pl.semaphore_wait(barrier, 2)

    @pl.when(full)
    def _():
        pl.semaphore_wait(barrier, 4)
        send_y()
        signal(ready_sem.at[2], z_prev)
        signal(ready_sem.at[3], z_next)

    @pl.when(even_row | full)
    def _():
        copies[2].start()
        copies[3].start()

    y_hi, y_lo = split(weights(iota((ny, ny), 0) - iota((ny, ny), 1)))
    z_hi, z_lo = split(weights(iota((nz, nz), 1) - iota((nz, nz), 0)))

    spread = jnp.where(which == 0, tail * powers(k + 1), 0.0)
    spread = jnp.where((which == 1) & (k == 0), edge, spread)
    spread = jnp.where(which == 8, -tail * powers(nz - k), spread)
    spread = jnp.where((which == 9) & (k == nz - 1), -edge, spread)
    spread_hi, spread_lo = split(spread)
    y_weight[:ny, :] = -tail * ratio * to_prev_y
    y_weight[ny:, :] = tail * ratio * to_next_y

    for p in range(planes):
        plane_hi = v_hi[p * ny:(p + 1) * ny, :]
        plane_lo = v_lo[p * ny:(p + 1) * ny, :]
        dy[p * ny:(p + 1) * ny, :] = dot(y_hi, plane_hi) + (dot(y_lo, plane_hi) + dot(y_hi, plane_lo))
    dz[...] = dot(v_hi, z_hi) + (dot(v_lo, z_hi) + dot(v_hi, z_lo))

    @pl.when(quick)
    def _():
        pl.semaphore_wait(ready_sem.at[2], 1)
        copies[2].start()
        pl.semaphore_wait(ready_sem.at[3], 1)
        copies[3].start()

    copies[2].wait_recv()
    copies[3].wait_recv()
    in_hi, in_lo = split(z_in[...])
    dz[...] += dot(
        jnp.concatenate([in_hi, in_lo, in_hi], axis=0),
        jnp.concatenate([spread_hi, spread_hi, spread_lo], axis=0),
        ((0,), (0,)),
    )

    @pl.when(even_row)
    def _():
        pl.semaphore_wait(ready_sem.at[0], 1)
        copies[0].start()
        pl.semaphore_wait(ready_sem.at[1], 1)
        copies[1].start()

    copies[0].wait_recv()
    copies[1].wait_recv()
    for copy in copies:
        copy.wait_send()


def finish(planes, own_y, dz, y_in, y_weight, dy_hbm, dz_hbm, dy, y_sem, z_sem):
    rows, nz = own_y.shape
    ny = rows // planes
    half = y_in.shape[0] // 2
    copies = []

    def store(source, target, p, sem):
        part = pl.ds(p * ny, ny)
        copies.append(pltpu.make_async_copy(source.at[part], target.at[part], sem.at[p]))
        copies[-1].start()

    copies.append(pltpu.make_async_copy(dz, dz_hbm, z_sem))
    copies[0].start()
    from_prev_y, from_next_y = y_weight[:ny, :], y_weight[ny:, :]
    first = jnp.where(iota((8, nz), 0) == 0, edge, 0.0)
    last = jnp.where(iota((8, nz), 0) == 7, -edge, 0.0)
    for p in range(planes):
        low = get_row(y_in, 0, planes, p, nz)
        low_edge = get_row(y_in, nz // 128 * planes, planes, p, nz)
        high = get_row(y_in, half, planes, p, nz)
        high_edge = get_row(y_in, half + nz // 128 * planes, planes, p, nz)
        part = slice(p * ny, (p + 1) * ny)
        dy[part, :] = own_y[part, :] + (from_prev_y * low + from_next_y * high)
        dy[p * ny:p * ny + 8, :] += first * low_edge
        dy[(p + 1) * ny - 8:(p + 1) * ny, :] += last * high_edge
        store(dy, dy_hbm, p, y_sem)
    for copy in copies:
        copy.wait()


def per_device(velocity):
    planes = velocity.shape[0] * velocity.shape[1]
    ny, nz = velocity.shape[2:]
    flat = (planes * ny, nz)
    half = (2 * planes * (nz // 128) + 7) // 8 * 8
    block = pltpu.VMEM(flat, jnp.float32)
    y_message = pltpu.VMEM((2 * half, 128), jnp.float32)
    z_message = pltpu.VMEM((16, planes * ny), jnp.float32)
    in_vmem = pl.BlockSpec(memory_space=pltpu.VMEM)
    in_hbm = pl.BlockSpec(memory_space=pltpu.HBM)
    parts = pl.pallas_call(
        functools.partial(exchange, planes),
        out_shape=(block, block, y_message, pltpu.VMEM((2 * ny, nz), jnp.float32)),
        in_specs=[in_hbm],
        out_specs=(in_vmem,) * 4,
        scratch_shapes=[
            block, y_message, z_message, z_message,
            pltpu.SemaphoreType.DMA((planes,)),
            pltpu.SemaphoreType.DMA((4,)),
            pltpu.SemaphoreType.DMA((4,)),
            pltpu.SemaphoreType.REGULAR((4,)),
        ],
        compiler_params=pltpu.CompilerParams(
            collective_id=0, has_side_effects=True, vmem_limit_bytes=16 * 2**20
        ),
    )(pltpu.with_memory_space_constraint(velocity.reshape(flat), pltpu.HBM))
    stored = pltpu.HBM(flat, jnp.float32)
    deriv_y, deriv_z = pl.pallas_call(
        functools.partial(finish, planes),
        out_shape=(stored, stored),
        in_specs=[in_vmem] * 4,
        out_specs=(in_hbm, in_hbm),
        scratch_shapes=[
            block,
            pltpu.SemaphoreType.DMA((planes,)),
            pltpu.SemaphoreType.DMA,
        ],
        compiler_params=pltpu.CompilerParams(vmem_limit_bytes=16 * 2**20),
    )(*(pltpu.with_memory_space_constraint(part, pltpu.VMEM) for part in parts))
    return deriv_y.reshape(velocity.shape), deriv_z.reshape(velocity.shape)


def solution(mesh):
    spec = P(None, None, "gy", "gz")
    return jax.shard_map(
        per_device, mesh=mesh, in_specs=(spec,), out_specs=(spec, spec), check_vma=False
    )
```

```python
import functools
import math

import jax
import jax.numpy as jnp
from jax import lax
from jax.experimental import pallas as pl
from jax.experimental.pallas import tpu as pltpu
from jax.sharding import PartitionSpec as P

MESH = pl.DeviceIdType.MESH
ratio = 1.5 - math.sqrt(5.0) / 2.0
near = 7.0 / 9.0
far = 1.0 / 36.0
green = 1.0 / (1.0 - 2.0 / 3.0 * ratio)
tail = green * (near * (1.0 / ratio - ratio) + far * (ratio**2 - 1.0 / ratio**2))
edge = far * green * (ratio - 1.0 / ratio)
log_ratio = math.log(ratio)


def powers(count):
    size = jnp.exp(count.astype(jnp.float32) * log_ratio)
    return jnp.where((count & 1) == 0, size, -size)


def weights(d):
    size = jnp.abs(d)
    value = tail * powers(size) + jnp.where(size == 1, edge, 0.0)
    return jnp.where(d > 0, value, jnp.where(d < 0, -value, 0.0))


def iota(shape, dim):
    return lax.broadcasted_iota(jnp.int32, shape, dim)


def split(x):
    high = x.astype(jnp.bfloat16)
    return high, (x - high.astype(jnp.float32)).astype(jnp.bfloat16)


def dot(a, b, dims=((1,), (0,))):
    return lax.dot_general(a, b, (dims, ((), ())), preferred_element_type=jnp.float32)


def put_row(ref, start, planes, p, row):
    for c in range(row.shape[1] // 128):
        place = start + c * planes + p
        ref[place:place + 1, :] = row[:, c * 128:(c + 1) * 128]


def get_row(ref, start, planes, p, nz):
    places = [start + c * planes + p for c in range(nz // 128)]
    return jnp.concatenate([ref[place:place + 1, :] for place in places], axis=1)


def exchange(planes, v_hbm, dy, dz, y_in, y_weight, v, y_out, z_out, z_in, load_sem, send_sem, recv_sem, ready_sem):
    rows, nz = v.shape
    ny = rows // planes
    half = y_out.shape[0] // 2
    gy, gz = lax.axis_size("gy"), lax.axis_size("gz")
    iy, iz = lax.axis_index("gy"), lax.axis_index("gz")
    y_next = (lax.rem(iy + 1, gy), iz)
    y_prev = (lax.rem(iy + gy - 1, gy), iz)
    z_next = (iy, lax.rem(iz + 1, gz))
    z_prev = (iy, lax.rem(iz + gz - 1, gz))

    odd_row = lax.rem(iy, 2) == 1
    even_row = lax.rem(iy, 2) == 0
    quick = odd_row & (lax.rem(iz, 2) == 0)
    full = odd_row & (lax.rem(iz, 2) == 1)
    barrier = pltpu.get_barrier_semaphore()

    def signal(sem, other):
        pl.semaphore_signal(sem, inc=1, device_id=other, device_id_type=MESH)

    @pl.when(even_row)
    def _():
        signal(barrier, y_prev)
        signal(barrier, y_next)

    @pl.when(even_row | quick)
    def _():
        signal(barrier, z_prev)
        signal(barrier, z_next)

    loads = []
    for p in range(planes):
        part = pl.ds(p * ny, ny)
        loads.append(pltpu.make_async_copy(v_hbm.at[part], v.at[part], load_sem.at[p]))
        loads[-1].start()

    def message_to(index, source, target, start, count, other):
        return pltpu.make_async_remote_copy(
            src_ref=source.at[pl.ds(start, count)],
            dst_ref=target.at[pl.ds(start, count)],
            send_sem=send_sem.at[index],
            recv_sem=recv_sem.at[index],
            device_id=other,
            device_id_type=MESH,
        )

    place = iota((ny, 128), 0)
    to_next_y = jnp.concatenate([powers(ny - 1 - place)] * (nz // 128), axis=1)
    to_prev_y = jnp.concatenate([powers(place)] * (nz // 128), axis=1)
    which, k = iota((16, nz), 0), iota((16, nz), 1)
    message = jnp.where(which == 0, powers(nz - 1 - k), 0.0)
    message = jnp.where((which == 1) & (k == nz - 1), 1.0, message)
    message = jnp.where(which == 8, powers(k), message)
    message = jnp.where((which == 9) & (k == 0), 1.0, message)
    message_hi, message_lo = split(message)
    message_both = jnp.concatenate([message_hi, message_lo], axis=0)
    if half > 2 * planes * (nz // 128):
        y_out[...] = jnp.zeros_like(y_out)
    for p in range(planes):
        loads[p].wait()
        plane = v[p * ny:(p + 1) * ny, :]
        put_row(y_out, 0, planes, p, jnp.sum(plane * to_next_y, axis=0, keepdims=True))
        put_row(y_out, nz // 128 * planes, planes, p, plane[ny - 1:ny, :])
    copies = [
        message_to(0, y_out, y_in, 0, half, y_next),
        message_to(1, y_out, y_in, half, half, y_prev),
        message_to(2, z_out, z_in, 0, 8, z_next),
        message_to(3, z_out, z_in, 8, 8, z_prev),
    ]

    def send_y_next():
        signal(ready_sem.at[1], y_next)
        copies[0].start()

    def send_y_prev():
        signal(ready_sem.at[0], y_prev)
        copies[1].start()

    @pl.when(quick)
    def _():
        pl.semaphore_wait(barrier, 2)
        send_y_next()

    for p in range(planes):
        plane = v[p * ny:(p + 1) * ny, :]
        put_row(y_out, half, planes, p, jnp.sum(plane * to_prev_y, axis=0, keepdims=True))
        put_row(y_out, half + nz // 128 * planes, planes, p, plane[0:1, :])

    @pl.when(quick)
    def _():
        send_y_prev()

    v_hi, v_lo = split(v[...])
    nt = ((1,), (1,))
    both = dot(message_both, v_hi, nt)
    z_out[...] = both[:16] + (both[16:] + dot(message_hi, v_lo, nt))

    @pl.when(even_row)
    def _():
        pl.semaphore_wait(barrier, 2)

    @pl.when(full)
    def _():
        pl.semaphore_wait(barrier, 4)
        send_y_next()
        send_y_prev()
        signal(ready_sem.at[2], z_prev)
        signal(ready_sem.at[3], z_next)

    @pl.when(even_row | full)
    def _():
        copies[2].start()
        copies[3].start()

    y_hi, y_lo = split(weights(iota((ny, ny), 0) - iota((ny, ny), 1)))
    z_hi, z_lo = split(weights(iota((nz, nz), 1) - iota((nz, nz), 0)))

    spread = jnp.where(which == 0, tail * powers(k + 1), 0.0)
    spread = jnp.where((which == 1) & (k == 0), edge, spread)
    spread = jnp.where(which == 8, -tail * powers(nz - k), spread)
    spread = jnp.where((which == 9) & (k == nz - 1), -edge, spread)
    spread_hi, spread_lo = split(spread)
    y_weight[:ny, :] = -tail * ratio * to_prev_y
    y_weight[ny:, :] = tail * ratio * to_next_y

    for p in range(planes):
        plane_hi = v_hi[p * ny:(p + 1) * ny, :]
        plane_lo = v_lo[p * ny:(p + 1) * ny, :]
        dy[p * ny:(p + 1) * ny, :] = dot(y_hi, plane_hi) + (dot(y_lo, plane_hi) + dot(y_hi, plane_lo))
    dz[...] = dot(v_hi, z_hi) + (dot(v_lo, z_hi) + dot(v_hi, z_lo))

    @pl.when(quick)
    def _():
        pl.semaphore_wait(ready_sem.at[2], 1)
        copies[2].start()
        pl.semaphore_wait(ready_sem.at[3], 1)
        copies[3].start()

    copies[2].wait_recv()
    copies[3].wait_recv()
    in_hi, in_lo = split(z_in[...])
    dz[...] += dot(
        jnp.concatenate([in_hi, in_lo, in_hi], axis=0),
        jnp.concatenate([spread_hi, spread_hi, spread_lo], axis=0),
        ((0,), (0,)),
    )

    @pl.when(even_row)
    def _():
        pl.semaphore_wait(ready_sem.at[0], 1)
        copies[0].start()
        pl.semaphore_wait(ready_sem.at[1], 1)
        copies[1].start()

    copies[0].wait_recv()
    copies[1].wait_recv()
    for copy in copies:
        copy.wait_send()


def finish(planes, own_y, dz, y_in, y_weight, dy_hbm, dz_hbm, dy, y_sem, z_sem):
    rows, nz = own_y.shape
    ny = rows // planes
    half = y_in.shape[0] // 2
    copies = []

    def store(source, target, p, sem):
        part = pl.ds(p * ny, ny)
        copies.append(pltpu.make_async_copy(source.at[part], target.at[part], sem.at[p]))
        copies[-1].start()

    copies.append(pltpu.make_async_copy(dz, dz_hbm, z_sem))
    copies[0].start()
    from_prev_y, from_next_y = y_weight[:ny, :], y_weight[ny:, :]
    first = jnp.where(iota((8, nz), 0) == 0, edge, 0.0)
    last = jnp.where(iota((8, nz), 0) == 7, -edge, 0.0)
    for p in range(planes):
        low = get_row(y_in, 0, planes, p, nz)
        low_edge = get_row(y_in, nz // 128 * planes, planes, p, nz)
        high = get_row(y_in, half, planes, p, nz)
        high_edge = get_row(y_in, half + nz // 128 * planes, planes, p, nz)
        part = slice(p * ny, (p + 1) * ny)
        dy[part, :] = own_y[part, :] + (from_prev_y * low + from_next_y * high)
        dy[p * ny:p * ny + 8, :] += first * low_edge
        dy[(p + 1) * ny - 8:(p + 1) * ny, :] += last * high_edge
        store(dy, dy_hbm, p, y_sem)
    for copy in copies:
        copy.wait()


def per_device(velocity):
    planes = velocity.shape[0] * velocity.shape[1]
    ny, nz = velocity.shape[2:]
    flat = (planes * ny, nz)
    half = (2 * planes * (nz // 128) + 7) // 8 * 8
    block = pltpu.VMEM(flat, jnp.float32)
    y_message = pltpu.VMEM((2 * half, 128), jnp.float32)
    z_message = pltpu.VMEM((16, planes * ny), jnp.float32)
    in_vmem = pl.BlockSpec(memory_space=pltpu.VMEM)
    in_hbm = pl.BlockSpec(memory_space=pltpu.HBM)
    parts = pl.pallas_call(
        functools.partial(exchange, planes),
        out_shape=(block, block, y_message, pltpu.VMEM((2 * ny, nz), jnp.float32)),
        in_specs=[in_hbm],
        out_specs=(in_vmem,) * 4,
        scratch_shapes=[
            block, y_message, z_message, z_message,
            pltpu.SemaphoreType.DMA((planes,)),
            pltpu.SemaphoreType.DMA((4,)),
            pltpu.SemaphoreType.DMA((4,)),
            pltpu.SemaphoreType.REGULAR((4,)),
        ],
        compiler_params=pltpu.CompilerParams(
            collective_id=0, has_side_effects=True, vmem_limit_bytes=16 * 2**20
        ),
    )(pltpu.with_memory_space_constraint(velocity.reshape(flat), pltpu.HBM))
    stored = pltpu.HBM(flat, jnp.float32)
    deriv_y, deriv_z = pl.pallas_call(
        functools.partial(finish, planes),
        out_shape=(stored, stored),
        in_specs=[in_vmem] * 4,
        out_specs=(in_hbm, in_hbm),
        scratch_shapes=[
            block,
            pltpu.SemaphoreType.DMA((planes,)),
            pltpu.SemaphoreType.DMA,
        ],
        compiler_params=pltpu.CompilerParams(vmem_limit_bytes=16 * 2**20),
    )(*(pltpu.with_memory_space_constraint(part, pltpu.VMEM) for part in parts))
    return deriv_y.reshape(velocity.shape), deriv_z.reshape(velocity.shape)


def solution(mesh):
    spec = P(None, None, "gy", "gz")
    return jax.shard_map(
        per_device, mesh=mesh, in_specs=(spec,), out_specs=(spec, spec), check_vma=False
    )
```
